128 devices in a mesh: replica: 8 (over z_lo, x), shard: 16 (over z_hi, y, core).
Axes of the slice: x: 4, y: 4, z: 4 (z_hi: 2, z_lo: 2; z = z_hi * 2 + z_lo), core: 2. Of those that a mesh axis runs over, the one named last changes fastest.
Arguments:
- tokens: bfloat16 [8, 4096, 12288], P('replica', 'shard'), may hold values from -6 to 6
- cotangent: bfloat16 [8, 4096, 12288], P('replica', 'shard'), may hold values from -6 to 6
- inner_up: float32 [8, 12288, 384], P('replica', 'shard'), may hold values from -5 to 5
- adam_first: float32 [8, 12288, 384], P('replica', 'shard'), may hold values from -4 to 4
- adam_second: float32 [8, 12288, 384], P('replica', 'shard'), may hold values from 0.05 to 2
- inner_down: bfloat16 [8, 12288, 384], P('replica', 'shard'), may hold values from -6 to 6
- down_accum: float32 [8, 12288, 384], P('replica', 'shard'), may hold values from -6 to 6
- anchor_up: float32 [12288, 384], P('shard'), may hold values from -5 to 5
- outer_momentum: float32 [12288, 384], P('shard'), may hold values from -4 to 4
Outputs:
- new_anchor: float32 [12288, 384], P('shard')
- new_momentum: float32 [12288, 384], P('shard')
- new_first: float32 [8, 12288, 384], P('replica', 'shard')
- new_second: float32 [8, 12288, 384], P('replica', 'shard')
- new_down_accum: float32 [8, 12288, 384], P('replica', 'shard')
The draws below stay inside these ranges and needn't reach their ends.
All inputs are finite; a program needn't handle non-finite values.
Results may differ from the reference program's by a relative error of at most 0.015.
Values may be sent and summed in bfloat16 or wider, within the bound.
A program may use at most 128 MiB of HBM per device.

```python
import math
import jax
import jax.numpy as jnp
from jax import lax

D = 12288
FFW = 384
TOK_DEV = 256
TOKR = 4096
N_REPLICA = 8
N_SHARD = 16


def common_field(key):
    return jnp.clip(jax.random.normal(key, (D, FFW), jnp.float32), -4.0, 4.0)


def offset_noise(key, shape, spread):
    return spread * jnp.clip(jax.random.normal(key, shape, jnp.float32), -4.0, 4.0)


def draw_inner_up(key, part):
    common = common_field(key)
    key = jax.random.fold_in(key, 11)
    spread = 0.05
    return common[None] + offset_noise(key, (N_REPLICA, D, FFW), spread)


def draw_anchor_up(key, part):
    common = common_field(key)
    key = jax.random.fold_in(key, 23)
    spread = 0.05
    return common + offset_noise(key, (D, FFW), spread)


def with_spikes(result, key, source, target, shards_of, factor):
    owner, partner = [(jnp.arange(result.shape[axis_at]) // (result.shape[axis_at] // shards_of)).reshape([-1 if axis == axis_at else 1 for axis in range(result.ndim)]) for axis_at in (source, target)]
    chosen = jax.random.permutation(key, shards_of)[partner]
    strong = (owner == chosen) | (owner == (partner + shards_of // 2) % shards_of)
    return jnp.where(strong, factor * result, result)


def block_levels(rng, shape, shards, smallest, high):
    factor_of = 1.0
    for position, parts in shards:
        steps = jax.random.uniform(jax.random.fold_in(jax.random.fold_in(rng, 6), position), (parts,), jnp.float32, smallest / len(shards), high / len(shards))
        factor_of = factor_of * jnp.repeat(jnp.exp(steps), shape[position] // parts).reshape((-1,) + (1,) * (len(shape) - 1 - position))
    return factor_of


def noise(rng, extent, scale, limit, cuts=(), held_as=jnp.bfloat16):
    entries = scale * jax.random.normal(rng, extent, jnp.float32)
    if cuts:
        entries = entries * block_levels(rng, extent, cuts, -0.22, 0.18)
    return jnp.clip(entries, -limit, limit).astype(held_as)


def bell_draw_with(key, dims, width, most, cuts, heavy, dtype=jnp.bfloat16):
    result = width * jax.random.normal(key, dims, jnp.float32)
    if cuts:
        result = result * block_levels(key, dims, cuts, -0.22, 0.18)
    return jnp.clip(with_spikes(result, jax.random.fold_in(key, 3), *heavy), -most, most).astype(dtype)


def setup_inputs(seed: int = 0) -> dict:
    streams_of = jax.random.split(jax.random.key(seed), 10)
    return {
        "tokens": bell_draw_with(streams_of[0], (N_REPLICA, TOKR, D), 1.0, 6.0, ((0, 8), (1, 16)), (1, 2, 16, 2.0)),
        "cotangent": bell_draw_with(streams_of[1], (N_REPLICA, TOKR, D), 1.0, 6.0, ((0, 8), (1, 16)), (1, 2, 16, 2.0)),
        "inner_up": draw_inner_up(jax.random.fold_in(streams_of[9], 71), 0),
        "adam_first": noise(streams_of[3], (N_REPLICA, D, FFW), 0.5, 4.0, ((0, 8), (1, 16)), jnp.float32),
        "adam_second": jnp.clip(jnp.exp(math.log(2.0) - 3.6888794 * jax.random.uniform(streams_of[4], (N_REPLICA, D, FFW), jnp.float32) ** block_levels(streams_of[4], (N_REPLICA, D, FFW), ((0, 8), (1, 16)), -0.2, 0.2)), 0.05, 2.0),
        "inner_down": noise(streams_of[5], (N_REPLICA, D, FFW), 1.0, 6.0, ((0, 8), (1, 16))),
        "down_accum": noise(streams_of[6], (N_REPLICA, D, FFW), 1.0, 6.0, ((0, 8), (1, 16)), jnp.float32),
        "anchor_up": draw_anchor_up(jax.random.fold_in(streams_of[9], 71), 0),
        "outer_momentum": noise(streams_of[8], (D, FFW), 0.5, 4.0, ((0, 16),), jnp.float32),
    }


beta_one = 0.8
beta_two = 0.95
inner_rate = 0.05
decay_rate = 0.1
adam_eps = 1e-08
adam_steps = 20
outer_mu = 0.9
outer_rate = 0.7

def activation(values):
    return jax.nn.gelu(values, approximate=True)

def replica_step(packed):
    inputs, upstream_grad, master_up, first_moment, second_moment, down_bf, accum_down = packed
    scale_in = D ** (-0.5)
    scale_hid = FFW ** (-0.5)
    up_bf = master_up.astype(jnp.bfloat16)
    pre_act = jnp.dot(inputs, up_bf, preferred_element_type=jnp.float32) * scale_in
    upstream = jnp.dot(upstream_grad, down_bf, preferred_element_type=jnp.float32) * scale_hid
    activated, pullback = jax.vjp(activation, pre_act)
    grad_pre = pullback(upstream)[0].astype(jnp.bfloat16)
    act_bf = activated.astype(jnp.bfloat16)
    group_in = inputs.reshape(N_SHARD, TOK_DEV, D)
    group_up = upstream_grad.reshape(N_SHARD, TOK_DEV, D)
    group_pre = grad_pre.reshape(N_SHARD, TOK_DEV, FFW)
    group_act = act_bf.reshape(N_SHARD, TOK_DEV, FFW)

    def add_group(carry, group):
        part_in, part_up, part_pre, part_act = group
        term_up = (jnp.dot(part_in.T, part_pre, preferred_element_type=jnp.float32) * scale_in).astype(jnp.bfloat16)
        term_down = (jnp.dot(part_up.T, part_act, preferred_element_type=jnp.float32) * scale_hid).astype(jnp.bfloat16)
        term_up, term_down = lax.optimization_barrier((term_up, term_down))
        return ((carry[0] + term_up.astype(jnp.float32), carry[1] + term_down.astype(jnp.float32)), None)
    zeros = jnp.zeros((D, FFW), jnp.float32)
    (up_grad, down_grad), _ = lax.scan(add_group, (zeros, zeros), (group_in, group_up, group_pre, group_act))
    new_first = beta_one * first_moment + (1.0 - beta_one) * up_grad
    new_second = beta_two * second_moment + (1.0 - beta_two) * up_grad * up_grad
    fix_one = 1.0 - beta_one ** adam_steps
    fix_two = 1.0 - beta_two ** adam_steps
    stepped = master_up - inner_rate * (new_first / fix_one / (jnp.sqrt(new_second / fix_two) + adam_eps) + decay_rate * master_up)
    return (stepped, new_first, new_second, accum_down + down_grad)

def reference(tokens, cotangent, inner_up, adam_first, adam_second, inner_down, down_accum, anchor_up, outer_momentum):
    stepped, new_first, new_second, new_down_accum = lax.map(replica_step, (tokens, cotangent, inner_up, adam_first, adam_second, inner_down, down_accum))
    pseudo_grad = (anchor_up[None] - stepped).astype(jnp.bfloat16)
    pseudo_grad = lax.optimization_barrier(pseudo_grad)
    outer_mean = lax.optimization_barrier(jnp.sum(pseudo_grad.astype(jnp.float32), axis=0)) / N_REPLICA
    new_momentum = outer_mu * outer_momentum + outer_mean
    new_anchor = anchor_up - outer_rate * (outer_mean + outer_mu * new_momentum)
    return (new_anchor, new_momentum, new_first, new_second, new_down_accum)
```

```python
import jax
import jax.numpy as jnp
from jax import lax
from jax.experimental import pallas as pl
from jax.experimental.pallas import tpu as pltpu
from jax.sharding import PartitionSpec as P

MESH = pl.DeviceIdType.MESH
D = 12288
FFW = 384
TOK = 256
ROWS = 768
CH = 256
NCH = 3
HALF = CH // 2
HALF_F = FFW // 2
N_REP = 8
PIECE = CH // N_REP

beta_one = 0.8
beta_two = 0.95
inner_rate = 0.05
decay_rate = 0.1
adam_eps = 1e-08
adam_steps = 20
outer_mu = 0.9
outer_rate = 0.7
fix_one = 1.0 - beta_one**adam_steps
fix_two = 1.0 - beta_two**adam_steps
GELU_K = 0.7978845608028654
GELU_C = 0.044715

F_UP, F_M1, F_M2, F_ACC, F_ANC, F_MOM = range(6)


def kernel(
    tok, cot, up, m1, m2, dn, acc, anc, mom,
    o_anc, o_mom, o_m1, o_m2, o_acc,
    X, W, A, R, G, T, B, F, PS, PR, MN,
    load_sem, out_sem, x_sem, xs_sem, xr_sem, ags, agr, rss, rsr, ps, pr, gs, gr, ars, arr, mns, mnr,
):
    rep = lax.axis_index("replica")
    shd = lax.axis_index("shard")
    x, zl = rep % 4, rep // 4
    c, y, zh = shd % 2, (shd // 2) % 4, shd // 8

    def shard_at(dy, dz, core):
        return ((zh + dz) % 2) * 8 + ((y + dy) % 4) * 2 + core

    partner = (rep, shard_at(0, 0, 1 - c))
    yp = (rep, shard_at(1, 0, c))
    ym = (rep, shard_at(3, 0, c))
    zp = (rep, shard_at(0, 1, c))

    def peer(p):
        return ((zl + p // 4) % 2) * 4 + (x + p % 4) % 4

    peers = [(peer(p), shd) for p in range(N_REP)]

    local = []
    for i, ref in enumerate((up.at[0], m1.at[0], m2.at[0], acc.at[0], anc, mom)):
        local.append(pltpu.make_async_copy(ref, F.at[i], load_sem.at[i]))
    dn_load = pltpu.make_async_copy(dn.at[0], W.at[1, 0], load_sem.at[6])
    local[F_UP].start()
    dn_load.start()

    barrier = pltpu.get_barrier_semaphore()
    others = [partner, yp, ym, zp] + peers[1:]
    for other in others:
        pl.semaphore_signal(barrier, inc=1, device_id=other, device_id_type=MESH)

    x_local = [[], []]
    for w, src in enumerate((tok, cot)):
        for s in range(8):
            columns = pl.ds(pl.multiple_of(shard_at(s % 4, s // 4, c) * ROWS, ROWS), ROWS)
            copy = pltpu.make_async_copy(src.at[0, :, columns], X.at[w, s, pl.ds(0, TOK)], x_sem.at[w, s])
            copy.start()
            x_local[w].append(copy)

    local[F_UP].wait()
    W[0, 0] = F[F_UP].astype(jnp.bfloat16)
    dn_load.wait()
    pl.semaphore_wait(barrier, len(others))

    sends = []

    def send(src, dst, s_sem, r_sem, to):
        copy = pltpu.make_async_remote_copy(
            src_ref=src, dst_ref=dst, send_sem=s_sem, recv_sem=r_sem, device_id=to, device_id_type=MESH
        )
        copy.start()
        sends.append(copy)
        return copy

    ag = {}

    def ag_send(w, j, k, from_slot, to_slot, first, count, to):
        rows = pl.ds(j * CH + first, count)
        ag[w, j, k] = send(W.at[w, from_slot, rows], W.at[w, to_slot, rows], ags.at[w, j, k], agr.at[w, j, k], to)

    def ag_own_z(w, j):
        ag_send(w, j, 2, 0, 4, 0, CH, zp)

    def ag_own_y(w, j):
        ag_send(w, j, 0, 0, 3, 0, CH, yp)
        ag_send(w, j, 1, 0, 1, 0, CH, ym)

    def ag_half(w, j):
        ag[w, j, 0].wait_recv()
        ag_send(w, j, 5, 3, 2, 0, HALF, yp)
        ag[w, j, 1].wait_recv()
        ag_send(w, j, 6, 1, 2, HALF, HALF, ym)

    def ag_far(w, j):
        ag[w, j, 2].wait_recv()
        ag_send(w, j, 3, 4, 7, 0, CH, yp)
        ag_send(w, j, 4, 4, 5, 0, CH, ym)

    def ag_last(w, j):
        ag[w, j, 5].wait_recv()
        ag[w, j, 6].wait_recv()
        ag_send(w, j, 7, 2, 6, 0, CH, zp)

    def ag_end(w, j):
        for k in (3, 4, 7):
            ag[w, j, k].wait_recv()

    def forward(w, j, slots, first):
        rows = pl.ds(j * CH, CH)

        @pl.loop(0, 4)
        def _(t):
            at = pl.ds(pl.multiple_of(t * 128, 128), 128)
            total = None if first else A[w, at]
            for s in slots:
                part = jnp.dot(X[w, s, at, rows], W[w, s, rows], preferred_element_type=jnp.float32)
                total = part if total is None else total + part
            A[w, at] = total

    for j in range(NCH):
        ag_own_z(0, j)
        ag_own_y(0, j)

    x_send = [[], []]
    for w, src in enumerate((tok, cot)):
        for s in range(8):
            columns = pl.ds(pl.multiple_of(shard_at(s % 4, s // 4, 1 - c) * ROWS, ROWS), ROWS)
            x_send[w].append(
                send(src.at[0, :, columns], X.at[w, s, pl.ds(TOK, TOK)], xs_sem.at[w, s], xr_sem.at[w, s], partner)
            )

    for j in range(NCH):
        ag_own_z(1, j)
    ag_half(0, 0)
    ag_far(0, 0)
    for s in range(8):
        x_local[0][s].wait()
        x_send[0][s].wait_recv()
    forward(0, 0, (0, 1, 3, 4), True)
    ag_half(0, 1)
    ag_far(0, 1)
    forward(0, 1, (0, 1, 3, 4), False)
    ag_half(0, 2)
    ag_far(0, 2)
    for j in range(NCH):
        ag_own_y(1, j)
    for i in (F_M1, F_M2, F_ACC, F_ANC, F_MOM):
        local[i].start()
    forward(0, 2, (0, 1, 3, 4), False)
    ag_last(0, 0)
    ag_last(0, 1)
    ag_end(0, 0)
    forward(0, 0, (2, 5, 6, 7), False)
    ag_last(0, 2)
    ag_end(0, 1)
    forward(0, 1, (2, 5, 6, 7), False)
    for s in range(8):
        x_local[1][s].wait()
        x_send[1][s].wait_recv()
    ag_half(1, 0)
    ag_far(1, 0)
    ag_end(0, 2)
    forward(0, 2, (2, 5, 6, 7), False)

    def swap_partial(w):
        return send(A.at[w, pl.ds(TOK, TOK)], R.at[w], ps.at[w], pr.at[w], partner)

    def swap_hidden(w):
        return send(G.at[w, 0], G.at[w, 1], gs.at[w], gr.at[w], partner)

    def terms(w, j):
        rows = pl.ds(j * CH, CH)
        scale = D ** (-0.5) if w == 0 else FFW ** (-0.5)

        @pl.loop(0, 8)
        def _(s):
            part = jnp.dot(G[w, 0], X[w, s, pl.ds(0, TOK), rows], preferred_element_type=jnp.float32)
            part += jnp.dot(G[w, 1], X[w, s, pl.ds(TOK, TOK), rows], preferred_element_type=jnp.float32)
            T[w, j, s] = (part * scale).astype(jnp.bfloat16)

    partial = swap_partial(0)
    forward(1, 0, (0, 1, 3, 4), True)
    ag_half(1, 1)
    ag_far(1, 1)
    partial.wait_recv()

    @pl.loop(0, 2)
    def _(t):
        at = pl.ds(pl.multiple_of(t * 128, 128), 128)
        v = (A[0, at] + R[0, at]) * D ** (-0.5)
        R[0, at] = v
        act = 0.5 * v * (1.0 + jnp.tanh(GELU_K * (v + GELU_C * (v * v * v))))
        G[1, 0, :, at] = act.T.astype(jnp.bfloat16)

    hidden = swap_hidden(1)
    forward(1, 1, (0, 1, 3, 4), False)
    ag_half(1, 2)
    ag_far(1, 2)
    hidden.wait_recv()
    terms(1, 0)
    forward(1, 2, (0, 1, 3, 4), False)
    ag_last(1, 0)
    terms(1, 1)
    ag_last(1, 1)
    ag_end(1, 0)
    forward(1, 0, (2, 5, 6, 7), False)
    terms(1, 2)
    ag_last(1, 2)
    ag_end(1, 1)
    forward(1, 1, (2, 5, 6, 7), False)

    rs = {}

    def rs_send(w, j, k, src, dst, to):
        rs[w, j, k] = send(src, dst, rss.at[w, j, k], rsr.at[w, j, k], to)

    def rs_one(w, j):
        rs_send(w, j, 0, T.at[w, j, 6], B.at[w, j, 0], zp)
        rs_send(w, j, 1, T.at[w, j, 5], B.at[w, j, 1], yp)
        rs_send(w, j, 2, T.at[w, j, 7], B.at[w, j, 2], ym)

    def add(w, j, slot, rows, *held):
        total = T[w, j, slot, rows].astype(jnp.float32)
        for k in held:
            total += B[w, j, k, rows].astype(jnp.float32)
        T[w, j, slot, rows] = total.astype(jnp.bfloat16)

    low, high, full = pl.ds(0, HALF_F), pl.ds(HALF_F, HALF_F), pl.ds(0, FFW)

    def rs_two(w, j):
        rs[w, j, 0].wait_recv()
        add(w, j, 2, full, 0)
        rs_send(w, j, 3, T.at[w, j, 2, low], B.at[w, j, 3, low], yp)
        rs_send(w, j, 4, T.at[w, j, 2, high], B.at[w, j, 3, high], ym)
        rs[w, j, 1].wait_recv()
        rs[w, j, 2].wait_recv()
        add(w, j, 4, full, 1, 2)
        rs_send(w, j, 5, T.at[w, j, 4], B.at[w, j, 4], zp)

    def rs_three(w, j):
        rs[w, j, 3].wait_recv()
        add(w, j, 1, low, 3)
        rs_send(w, j, 6, T.at[w, j, 1], B.at[w, j, 5], yp)
        rs[w, j, 4].wait_recv()
        add(w, j, 3, high, 3)
        rs_send(w, j, 7, T.at[w, j, 3], B.at[w, j, 6], ym)

    def rs_four(w, j):
        for k in (5, 6, 7):
            rs[w, j, k].wait_recv()
        total = T[w, j, 0].astype(jnp.float32)
        for k in (4, 5, 6):
            total += B[w, j, k].astype(jnp.float32)
        return total.T

    rs_one(1, 0)
    ag_end(1, 2)
    forward(1, 2, (2, 5, 6, 7), False)
    partial = swap_partial(1)
    partial.wait_recv()

    @pl.loop(0, 2)
    def _(t):
        at = pl.ds(pl.multiple_of(t * 128, 128), 128)
        upstream = (A[1, at] + R[1, at]) * FFW ** (-0.5)
        v = R[0, at]
        squared = v * v
        th = jnp.tanh(GELU_K * (v + GELU_C * (v * squared)))
        slope = 0.5 * (1.0 + th) + 0.5 * v * (1.0 - th * th) * (GELU_K * (1.0 + 3.0 * GELU_C * squared))
        G[0, 0, :, at] = (upstream * slope).T.astype(jnp.bfloat16)

    hidden = swap_hidden(0)
    hidden.wait_recv()
    for j in range(NCH):
        terms(0, j)
        rs_one(0, j)
    rs_one(1, 1)
    rs_one(1, 2)
    rs_two(1, 0)
    for j in range(NCH):
        rs_two(0, j)
    rs_two(1, 1)
    rs_two(1, 2)
    for i in (F_M1, F_M2, F_ACC, F_ANC, F_MOM):
        local[i].wait()

    outs = []

    def put(i, ref, j):
        rows = pl.ds(j * CH, CH)
        copy = pltpu.make_async_copy(F.at[i, rows], ref.at[rows], out_sem.at[i - 1, j])
        copy.start()
        outs.append(copy)

    ar = {}

    def adam(j):
        rows = pl.ds(j * CH, CH)
        grad = rs_four(0, j)
        first = beta_one * F[F_M1, rows] + (1.0 - beta_one) * grad
        F[F_M1, rows] = first
        second = beta_two * F[F_M2, rows] + (1.0 - beta_two) * grad * grad
        F[F_M2, rows] = second
        master = F[F_UP, rows]
        stepped = master - inner_rate * (
            first / fix_one / (jnp.sqrt(second / fix_two) + adam_eps) + decay_rate * master
        )
        PS[j] = (F[F_ANC, rows] - stepped).astype(jnp.bfloat16)
        for p in range(1, N_REP):
            piece = pl.ds(pl.multiple_of(peers[p][0] * PIECE, PIECE), PIECE)
            back = (p // 4) * 4 + (-p) % 4
            ar[j, p] = send(PS.at[j, piece], PR.at[j, back], ars.at[j, p - 1], arr.at[j, back - 1], peers[p])
        put(F_M1, o_m1.at[0], j)
        put(F_M2, o_m2.at[0], j)

    mean = {}

    def reduce_mean(j):
        mine = pl.ds(pl.multiple_of(rep * PIECE, PIECE), PIECE)
        total = PS[j, mine].astype(jnp.float32)
        for p in range(1, N_REP):
            ar[j, p].wait_recv()
        for p in range(1, N_REP):
            total += PR[j, p].astype(jnp.float32)
        MN[j, mine] = (total / N_REP).astype(jnp.bfloat16)
        for p in range(1, N_REP):
            back = (p // 4) * 4 + (-p) % 4
            mean[j, p] = send(MN.at[j, mine], MN.at[j, mine], mns.at[j, p - 1], mnr.at[j, back - 1], peers[p])

    def outer(j):
        rows = pl.ds(j * CH, CH)
        for p in range(1, N_REP):
            mean[j, p].wait_recv()
        outer_mean = MN[j].astype(jnp.float32)
        new_momentum = outer_mu * F[F_MOM, rows] + outer_mean
        F[F_MOM, rows] = new_momentum
        F[F_ANC, rows] = F[F_ANC, rows] - outer_rate * (outer_mean + outer_mu * new_momentum)
        put(F_MOM, o_mom, j)
        put(F_ANC, o_anc, j)

    def down(j):
        rows = pl.ds(j * CH, CH)
        F[F_ACC, rows] = F[F_ACC, rows] + rs_four(1, j)
        put(F_ACC, o_acc.at[0], j)

    for j in range(NCH):
        rs_three(0, j)
    rs_three(1, 0)
    adam(0)
    rs_three(1, 1)
    adam(1)
    rs_three(1, 2)
    adam(2)
    for j in range(NCH):
        reduce_mean(j)
    down(0)
    down(1)
    for j in range(NCH):
        outer(j)
    down(2)
    for copy in sends:
        copy.wait_send()
    for copy in outs:
        copy.wait()


def on_device(tokens, cotangent, inner_up, adam_first, adam_second, inner_down, down_accum, anchor_up, outer_momentum):
    flat = jax.ShapeDtypeStruct((ROWS, FFW), jnp.float32)
    deep = jax.ShapeDtypeStruct((1, ROWS, FFW), jnp.float32)
    dma = pltpu.SemaphoreType.DMA
    bf16, f32 = jnp.bfloat16, jnp.float32
    return pl.pallas_call(
        kernel,
        out_shape=(flat, flat, deep, deep, deep),
        in_specs=[pl.BlockSpec(memory_space=pl.ANY)] * 9,
        out_specs=[pl.BlockSpec(memory_space=pl.ANY)] * 5,
        scratch_shapes=[
            pltpu.VMEM((2, 8, 2 * TOK, ROWS), bf16),
            pltpu.VMEM((2, 8, ROWS, FFW), bf16),
            pltpu.VMEM((2, 2 * TOK, FFW), f32),
            pltpu.VMEM((2, TOK, FFW), f32),
            pltpu.VMEM((2, 2, FFW, TOK), bf16),
            pltpu.VMEM((2, NCH, 8, FFW, CH), bf16),
            pltpu.VMEM((2, NCH, 7, FFW, CH), bf16),
            pltpu.VMEM((6, ROWS, FFW), f32),
            pltpu.VMEM((NCH, CH, FFW), bf16),
            pltpu.VMEM((NCH, N_REP, PIECE, FFW), bf16),
            pltpu.VMEM((NCH, CH, FFW), bf16),
            dma((7,)),
            dma((5, NCH)),
            dma((2, 8)),
            dma((2, 8)),
            dma((2, 8)),
            dma((2, NCH, 8)),
            dma((2, NCH, 8)),
            dma((2, NCH, 8)),
            dma((2, NCH, 8)),
            dma((2,)),
            dma((2,)),
            dma((2,)),
            dma((2,)),
            dma((NCH, N_REP - 1)),
            dma((NCH, N_REP - 1)),
            dma((NCH, N_REP - 1)),
            dma((NCH, N_REP - 1)),
        ],
        name="window",
        compiler_params=pltpu.CompilerParams(
            collective_id=0, has_side_effects=True, vmem_limit_bytes=58 * 2**20
        ),
        cost_estimate=pl.CostEstimate(flops=9_700_000_000, bytes_accessed=30_000_000, transcendentals=200_000),
    )(tokens, cotangent, inner_up, adam_first, adam_second, inner_down, down_accum, anchor_up, outer_momentum)


def solution(mesh):
    return jax.shard_map(
        on_device,
        mesh=mesh,
        in_specs=(
            P("replica", "shard", None),
            P("replica", "shard", None),
            P("replica", "shard", None),
            P("replica", "shard", None),
            P("replica", "shard", None),
            P("replica", "shard", None),
            P("replica", "shard", None),
            P("shard", None),
            P("shard", None),
        ),
        out_specs=(
            P("shard", None),
            P("shard", None),
            P("replica", "shard", None),
            P("replica", "shard", None),
            P("replica", "shard", None),
        ),
        check_vma=False,
    )
```

```python
import jax
import jax.numpy as jnp
from jax import lax
from jax.experimental import pallas as pl
from jax.experimental.pallas import tpu as pltpu
from jax.sharding import PartitionSpec as P

MESH = pl.DeviceIdType.MESH
D = 12288
FFW = 384
TOK = 256
ROWS = 768
CH = 256
NCH = 3
HALF = CH // 2
HALF_F = FFW // 2
N_REP = 8
PIECE = CH // N_REP
BY_Z_AG = (0,)
BY_Z_RS = ()

beta_one = 0.8
beta_two = 0.95
inner_rate = 0.05
decay_rate = 0.1
adam_eps = 1e-08
adam_steps = 20
outer_mu = 0.9
outer_rate = 0.7
fix_one = 1.0 - beta_one**adam_steps
fix_two = 1.0 - beta_two**adam_steps
GELU_K = 0.7978845608028654
GELU_C = 0.044715


def kernel(
    tok, cot, up, m1, m2, dn, acc, anc, mom,
    o_anc, o_mom, o_m1, o_m2, o_acc,
    X, W, A, R, G, T, B, U, PS, PR, MN,
    load_sem, x_sem, xs_sem, xr_sem, ags, agr, rss, rsr, ps, pr, gs, gr, ars, arr, mns, mnr,
):
    rep = lax.axis_index("replica")
    shd = lax.axis_index("shard")
    x, zl = rep % 4, rep // 4
    c, y, zh = shd % 2, (shd // 2) % 4, shd // 8

    def shard_at(dy, dz, core):
        return ((zh + dz) % 2) * 8 + ((y + dy) % 4) * 2 + core

    partner = (rep, shard_at(0, 0, 1 - c))
    yp = (rep, shard_at(1, 0, c))
    ym = (rep, shard_at(3, 0, c))
    zp = (rep, shard_at(0, 1, c))

    def peer(p):
        return ((zl + p // 4) % 2) * 4 + (x + p % 4) % 4

    peers = [(peer(p), shd) for p in range(N_REP)]

    barrier = pltpu.get_barrier_semaphore()
    others = [partner, yp, ym, zp] + peers[1:]
    for other in others:
        pl.semaphore_signal(barrier, inc=1, device_id=other, device_id_type=MESH)

    chunk = [pl.ds(j * CH, CH) for j in range(NCH)]
    up_load = [pltpu.make_async_copy(up.at[0, chunk[j]], U.at[chunk[j]], load_sem.at[j]) for j in range(NCH)]
    for copy in up_load:
        copy.start()
    dn_load = pltpu.make_async_copy(dn.at[0], W.at[1, 0], load_sem.at[3])
    late = [
        pltpu.make_async_copy(src, dst, load_sem.at[4 + i])
        for i, (src, dst) in enumerate(((m1.at[0], o_m1), (m2.at[0], o_m2), (acc.at[0], o_acc), (anc, o_anc), (mom, o_mom)))
    ]
    pl.semaphore_wait(barrier, len(others))

    sends = []

    def send(src, dst, s_sem, r_sem, to):
        copy = pltpu.make_async_remote_copy(
            src_ref=src, dst_ref=dst, send_sem=s_sem, recv_sem=r_sem, device_id=to, device_id_type=MESH
        )
        copy.start()
        sends.append(copy)
        return copy

    ag = {}

    def ag_send(w, j, k, from_slot, to_slot, first, count, to):
        rows = pl.ds(j * CH + first, count)
        src = dn.at[0, rows] if w == 1 and from_slot == 0 else W.at[w, from_slot, rows]
        ag[w, j, k] = send(src, W.at[w, to_slot, rows], ags.at[w, j, k], agr.at[w, j, k], to)

    def ag_own_z(w, j):
        ag_send(w, j, 2, 0, 4, 0, CH, zp)

    def ag_own_y(w, j):
        ag_send(w, j, 0, 0, 3, 0, CH, yp)
        ag_send(w, j, 1, 0, 1, 0, CH, ym)

    def ag_half(w, j):
        ag[w, j, 0].wait_recv()
        ag_send(w, j, 5, 3, 2, 0, HALF, yp)
        if j in BY_Z_AG:
            ag_send(w, j, 8, 3, 7, HALF, HALF, zp)
        ag[w, j, 1].wait_recv()
        ag_send(w, j, 6, 1, 2, HALF, HALF, ym)
        if j in BY_Z_AG:
            ag_send(w, j, 9, 1, 5, HALF, HALF, zp)

    def ag_far(w, j):
        ag[w, j, 2].wait_recv()
        count = HALF if j in BY_Z_AG else CH
        ag_send(w, j, 3, 4, 7, 0, count, yp)
        ag_send(w, j, 4, 4, 5, 0, count, ym)

    def ag_last(w, j):
        ag[w, j, 5].wait_recv()
        ag[w, j, 6].wait_recv()
        ag_send(w, j, 7, 2, 6, 0, CH, zp)

    def ag_end(w, j):
        for k in (3, 4, 7, 8, 9) if j in BY_Z_AG else (3, 4, 7):
            ag[w, j, k].wait_recv()

    def forward(w, j, slots, first):
        rows = pl.ds(j * CH, CH)

        @pl.loop(0, 4)
        def _(t):
            at = pl.ds(pl.multiple_of(t * 128, 128), 128)
            total = None if first else A[w, at]
            for s in slots:
                part = jnp.dot(X[w, s, at, rows], W[w, s, rows], preferred_element_type=jnp.float32)
                total = part if total is None else total + part
            A[w, at] = total

    ag_own_z(1, 0)
    ag_own_y(1, 0)
    for j in range(NCH):
        up_load[j].wait()
        W[0, 0, chunk[j]] = U[chunk[j]].astype(jnp.bfloat16)
        ag_own_z(0, j)
        ag_own_y(0, j)

    x_local, x_send = [[], []], [[], []]
    for w, src in enumerate((tok, cot)):
        for s in range(8):
            mine = pl.ds(pl.multiple_of(shard_at(s % 4, s // 4, c) * ROWS, ROWS), ROWS)
            its = pl.ds(pl.multiple_of(shard_at(s % 4, s // 4, 1 - c) * ROWS, ROWS), ROWS)
            copy = pltpu.make_async_copy(src.at[0, :, mine], X.at[w, s, pl.ds(0, TOK)], x_sem.at[w, s])
            copy.start()
            x_local[w].append(copy)
            x_send[w].append(
                send(src.at[0, :, its], X.at[w, s, pl.ds(TOK, TOK)], xs_sem.at[w, s], xr_sem.at[w, s], partner)
            )
    dn_load.start()

    def x_wait(w):
        for s in range(8):
            x_local[w][s].wait()
            x_send[w][s].wait_recv()

    near, far = (0, 1, 3, 4), (2, 5, 6, 7)
    ag_own_z(1, 1)
    ag_own_z(1, 2)
    ag_half(1, 0)
    ag_far(1, 0)
    ag_half(0, 0)
    ag_far(0, 0)
    ag_own_y(1, 1)
    x_wait(0)
    forward(0, 0, near, True)
    ag_half(0, 1)
    ag_far(0, 1)
    ag_own_y(1, 2)
    ag_last(1, 0)
    ag_last(0, 0)
    forward(0, 1, near, False)
    ag_half(0, 2)
    ag_far(0, 2)
    for copy in late:
        copy.start()
    forward(0, 2, near, False)
    ag_last(0, 1)
    ag_end(0, 0)
    forward(0, 0, far, False)
    ag_half(1, 1)
    ag_far(1, 1)
    ag_last(0, 2)
    ag_end(0, 1)
    forward(0, 1, far, False)
    ag_half(1, 2)
    ag_far(1, 2)
    ag_end(0, 2)
    forward(0, 2, far, False)

    def swap_partial(w):
        return send(A.at[w, pl.ds(TOK, TOK)], R.at[w], ps.at[w], pr.at[w], partner)

    def swap_hidden(w):
        return send(G.at[w, 0], G.at[w, 1], gs.at[w], gr.at[w], partner)

    def terms(w, j):
        rows = pl.ds(j * CH, CH)
        scale = D ** (-0.5) if w == 0 else FFW ** (-0.5)

        @pl.loop(0, 8)
        def _(s):
            part = jnp.dot(G[w, 0], X[w, s, pl.ds(0, TOK), rows], preferred_element_type=jnp.float32)
            part += jnp.dot(G[w, 1], X[w, s, pl.ds(TOK, TOK), rows], preferred_element_type=jnp.float32)
            T[w, j, s] = (part * scale).astype(jnp.bfloat16)

    partial = swap_partial(0)
    x_wait(1)
    dn_load.wait()
    forward(1, 0, near, True)
    ag_last(1, 1)
    partial.wait_recv()

    @pl.loop(0, 2)
    def _(t):
        at = pl.ds(pl.multiple_of(t * 128, 128), 128)
        v = (A[0, at] + R[0, at]) * D ** (-0.5)
        R[0, at] = v
        act = 0.5 * v * (1.0 + jnp.tanh(GELU_K * (v + GELU_C * (v * v * v))))
        G[1, 0, :, at] = act.T.astype(jnp.bfloat16)

    hidden = swap_hidden(1)
    rs = {}

    def rs_send(w, j, k, src, dst, to):
        rs[w, j, k] = send(src, dst, rss.at[w, j, k], rsr.at[w, j, k], to)

    low, high, full = pl.ds(0, HALF_F), pl.ds(HALF_F, HALF_F), pl.ds(0, FFW)

    def rs_one(w, j):
        by_z = j in BY_Z_RS
        to_yp, to_ym = (low, high) if by_z else (full, full)
        rs_send(w, j, 0, T.at[w, j, 6], B.at[w, j, 0], zp)
        rs_send(w, j, 1, T.at[w, j, 5, to_yp], B.at[w, j, 1, to_yp], yp)
        rs_send(w, j, 2, T.at[w, j, 7, to_ym], B.at[w, j, 2, to_ym], ym)
        if by_z:
            rs_send(w, j, 8, T.at[w, j, 5, high], B.at[w, j, 7, high], zp)
            rs_send(w, j, 9, T.at[w, j, 7, low], B.at[w, j, 7, low], zp)

    def add(w, j, slot, rows, *held):
        total = T[w, j, slot, rows].astype(jnp.float32)
        for k in held:
            total += B[w, j, k, rows].astype(jnp.float32)
        T[w, j, slot, rows] = total.astype(jnp.bfloat16)

    def rs_two(w, j):
        rs[w, j, 0].wait_recv()
        add(w, j, 2, full, 0)
        rs_send(w, j, 3, T.at[w, j, 2, low], B.at[w, j, 3, low], yp)
        rs_send(w, j, 4, T.at[w, j, 2, high], B.at[w, j, 3, high], ym)
        rs[w, j, 1].wait_recv()
        rs[w, j, 2].wait_recv()
        if j in BY_Z_RS:
            add(w, j, 4, low, 1)
            add(w, j, 4, high, 2)
        else:
            add(w, j, 4, full, 1, 2)
        rs_send(w, j, 5, T.at[w, j, 4], B.at[w, j, 4], zp)

    def rs_three(w, j):
        by_z = j in BY_Z_RS
        rs[w, j, 3].wait_recv()
        add(w, j, 1, low, 3)
        if by_z:
            rs[w, j, 8].wait_recv()
            add(w, j, 1, high, 7)
        rs_send(w, j, 6, T.at[w, j, 1], B.at[w, j, 5], yp)
        rs[w, j, 4].wait_recv()
        add(w, j, 3, high, 3)
        if by_z:
            rs[w, j, 9].wait_recv()
            add(w, j, 3, low, 7)
        rs_send(w, j, 7, T.at[w, j, 3], B.at[w, j, 6], ym)

    def rs_four(w, j):
        for k in (5, 6, 7):
            rs[w, j, k].wait_recv()
        total = T[w, j, 0].astype(jnp.float32)
        for k in (4, 5, 6):
            total += B[w, j, k].astype(jnp.float32)
        return total.T

    ag_end(1, 0)
    forward(1, 0, far, False)
    forward(1, 1, near, False)
    hidden.wait_recv()
    terms(1, 0)
    ag_last(1, 2)
    rs_one(1, 0)
    forward(1, 2, near, False)
    terms(1, 1)
    rs_one(1, 1)
    terms(1, 2)
    rs_one(1, 2)
    ag_end(1, 1)
    forward(1, 1, far, False)
    ag_end(1, 2)
    forward(1, 2, far, False)
    partial = swap_partial(1)
    partial.wait_recv()

    @pl.loop(0, 2)
    def _(t):
        at = pl.ds(pl.multiple_of(t * 128, 128), 128)
        upstream = (A[1, at] + R[1, at]) * FFW ** (-0.5)
        v = R[0, at]
        squared = v * v
        th = jnp.tanh(GELU_K * (v + GELU_C * (v * squared)))
        slope = 0.5 * (1.0 + th) + 0.5 * v * (1.0 - th * th) * (GELU_K * (1.0 + 3.0 * GELU_C * squared))
        G[0, 0, :, at] = (upstream * slope).T.astype(jnp.bfloat16)

    hidden = swap_hidden(0)
    hidden.wait_recv()
    for j in range(NCH):
        terms(0, j)
        rs_one(0, j)
        rs_two(1, j)
    for j in range(NCH):
        rs_two(0, j)
    for copy in late:
        copy.wait()

    ar = {}

    def adam(j):
        rows = pl.ds(j * CH, CH)
        grad = rs_four(0, j)
        first = beta_one * o_m1[rows] + (1.0 - beta_one) * grad
        o_m1[rows] = first
        second = beta_two * o_m2[rows] + (1.0 - beta_two) * grad * grad
        o_m2[rows] = second
        master = U[rows]
        stepped = master - inner_rate * (
            first / fix_one / (jnp.sqrt(second / fix_two) + adam_eps) + decay_rate * master
        )
        PS[j] = (o_anc[rows] - stepped).astype(jnp.bfloat16)
        for p in range(1, N_REP):
            piece = pl.ds(pl.multiple_of(peers[p][0] * PIECE, PIECE), PIECE)
            back = (p // 4) * 4 + (-p) % 4
            ar[j, p] = send(PS.at[j, piece], PR.at[j, back], ars.at[j, p - 1], arr.at[j, back - 1], peers[p])

    mean = {}

    def reduce_mean(j):
        mine = pl.ds(pl.multiple_of(rep * PIECE, PIECE), PIECE)
        total = PS[j, mine].astype(jnp.float32)
        for p in range(1, N_REP):
            ar[j, p].wait_recv()
        for p in range(1, N_REP):
            total += PR[j, p].astype(jnp.float32)
        MN[j, mine] = (total / N_REP).astype(jnp.bfloat16)
        for p in range(1, N_REP):
            back = (p // 4) * 4 + (-p) % 4
            mean[j, p] = send(MN.at[j, mine], MN.at[j, mine], mns.at[j, p - 1], mnr.at[j, back - 1], peers[p])

    def outer(j):
        rows = pl.ds(j * CH, CH)
        for p in range(1, N_REP):
            mean[j, p].wait_recv()
        outer_mean = MN[j].astype(jnp.float32)
        new_momentum = outer_mu * o_mom[rows] + outer_mean
        o_mom[rows] = new_momentum
        o_anc[rows] = o_anc[rows] - outer_rate * (outer_mean + outer_mu * new_momentum)

    def down(j):
        rows = pl.ds(j * CH, CH)
        o_acc[rows] = o_acc[rows] + rs_four(1, j)

    for j in range(NCH):
        rs_three(0, j)
    rs_three(1, 0)
    adam(0)
    rs_three(1, 1)
    adam(1)
    rs_three(1, 2)
    adam(2)
    for j in range(NCH):
        reduce_mean(j)
    down(0)
    down(1)
    for j in range(NCH):
        outer(j)
    down(2)
    for copy in sends:
        copy.wait_send()


def place(anc, mom, m1, m2, acc, o_anc, o_mom, o_m1, o_m2, o_acc, sem):
    pairs = ((anc, o_anc), (mom, o_mom), (m1, o_m1.at[0]), (m2, o_m2.at[0]), (acc, o_acc.at[0]))
    copies = [pltpu.make_async_copy(src, dst, sem.at[i]) for i, (src, dst) in enumerate(pairs)]
    for copy in copies:
        copy.start()
    for copy in copies:
        copy.wait()


def on_device(tokens, cotangent, inner_up, adam_first, adam_second, inner_down, down_accum, anchor_up, outer_momentum):
    flat = jax.ShapeDtypeStruct((ROWS, FFW), jnp.float32)
    deep = jax.ShapeDtypeStruct((1, ROWS, FFW), jnp.float32)
    dma = pltpu.SemaphoreType.DMA
    bf16, f32 = jnp.bfloat16, jnp.float32
    held = pl.pallas_call(
        kernel,
        out_shape=(pltpu.VMEM((ROWS, FFW), f32),) * 5,
        in_specs=[pl.BlockSpec(memory_space=pl.ANY)] * 9,
        out_specs=[pl.BlockSpec(memory_space=pltpu.VMEM)] * 5,
        scratch_shapes=[
            pltpu.VMEM((2, 8, 2 * TOK, ROWS), bf16),
            pltpu.VMEM((2, 8, ROWS, FFW), bf16),
            pltpu.VMEM((2, 2 * TOK, FFW), f32),
            pltpu.VMEM((2, TOK, FFW), f32),
            pltpu.VMEM((2, 2, FFW, TOK), bf16),
            pltpu.VMEM((2, NCH, 8, FFW, CH), bf16),
            pltpu.VMEM((2, NCH, 8, FFW, CH), bf16),
            pltpu.VMEM((ROWS, FFW), f32),
            pltpu.VMEM((NCH, CH, FFW), bf16),
            pltpu.VMEM((NCH, N_REP, PIECE, FFW), bf16),
            pltpu.VMEM((NCH, CH, FFW), bf16),
            dma((9,)),
            dma((2, 8)),
            dma((2, 8)),
            dma((2, 8)),
            dma((2, NCH, 10)),
            dma((2, NCH, 10)),
            dma((2, NCH, 10)),
            dma((2, NCH, 10)),
            dma((2,)),
            dma((2,)),
            dma((2,)),
            dma((2,)),
            dma((NCH, N_REP - 1)),
            dma((NCH, N_REP - 1)),
            dma((NCH, N_REP - 1)),
            dma((NCH, N_REP - 1)),
        ],
        name="window",
        compiler_params=pltpu.CompilerParams(
            collective_id=0, has_side_effects=True, vmem_limit_bytes=52 * 2**20
        ),
        cost_estimate=pl.CostEstimate(flops=9_700_000_000, bytes_accessed=30_000_000, transcendentals=200_000),
    )(tokens, cotangent, inner_up, adam_first, adam_second, inner_down, down_accum, anchor_up, outer_momentum)
    return pl.pallas_call(
        place,
        out_shape=(flat, flat, deep, deep, deep),
        in_specs=[pl.BlockSpec(memory_space=pltpu.VMEM)] * 5,
        out_specs=[pl.BlockSpec(memory_space=pl.ANY)] * 5,
        scratch_shapes=[dma((5,))],
        name="place",
        compiler_params=pltpu.CompilerParams(vmem_limit_bytes=2**20),
    )(*(pltpu.with_memory_space_constraint(value, pltpu.VMEM) for value in held))


def solution(mesh):
    return jax.shard_map(
        on_device,
        mesh=mesh,
        in_specs=(
            P("replica", "shard", None),
            P("replica", "shard", None),
            P("replica", "shard", None),
            P("replica", "shard", None),
            P("replica", "shard", None),
            P("replica", "shard", None),
            P("replica", "shard", None),
            P("shard", None),
            P("shard", None),
        ),
        out_specs=(
            P("shard", None),
            P("shard", None),
            P("replica", "shard", None),
            P("replica", "shard", None),
            P("replica", "shard", None),
        ),
        check_vma=False,
    )
```

```python
import jax
import jax.numpy as jnp
from jax import lax
from jax.experimental import pallas as pl
from jax.experimental.pallas import tpu as pltpu
from jax.sharding import PartitionSpec as P

MESH = pl.DeviceIdType.MESH
D = 12288
FFW = 384
TOK = 256
ROWS = 768
CH = 256
NCH = 3
HALF = CH // 2
HALF_F = FFW // 2
N_REP = 8
N_X = 4
PIECE = CH // N_X
BY_Z_AG = ((0, 1), (0, 2))
BY_Z_RS = ((0, 0),)

beta_one = 0.8
beta_two = 0.95
inner_rate = 0.05
decay_rate = 0.1
adam_eps = 1e-08
adam_steps = 20
outer_mu = 0.9
outer_rate = 0.7
fix_one = 1.0 - beta_one**adam_steps
fix_two = 1.0 - beta_two**adam_steps
GELU_K = 0.7978845608028654
GELU_C = 0.044715


def kernel(
    tok, cot, up, m1, m2, dn, acc, anc, mom,
    o_anc, o_mom, o_m1, o_m2, o_acc,
    X, W, A, R, G, T, B, U, PS, PR, MN,
    load_sem, x_sem, xs_sem, xr_sem, ags, agr, rss, rsr, ps, pr, gs, gr, ars, arr, mns, mnr,
):
    rep = lax.axis_index("replica")
    shd = lax.axis_index("shard")
    x, zl = rep % 4, rep // 4
    c, y, zh = shd % 2, (shd // 2) % 4, shd // 8

    def shard_at(dy, dz, core):
        return ((zh + dz) % 2) * 8 + ((y + dy) % 4) * 2 + core

    partner = (rep, shard_at(0, 0, 1 - c))
    yp = (rep, shard_at(1, 0, c))
    ym = (rep, shard_at(3, 0, c))
    zp = (rep, shard_at(0, 1, c))

    beside = [(zl * 4 + (x + p) % 4, shd) for p in range(4)]
    above = ((1 - zl) * 4 + x, shd)

    barrier = pltpu.get_barrier_semaphore()
    others = [partner, yp, ym, zp, above] + beside[1:]
    for other in others:
        pl.semaphore_signal(barrier, inc=1, device_id=other, device_id_type=MESH)

    chunk = [pl.ds(j * CH, CH) for j in range(NCH)]
    up_load = [pltpu.make_async_copy(up.at[0, chunk[j]], U.at[chunk[j]], load_sem.at[j]) for j in range(NCH)]
    for copy in up_load:
        copy.start()
    dn_load = pltpu.make_async_copy(dn.at[0], W.at[1, 0], load_sem.at[3])
    late = [
        pltpu.make_async_copy(src, dst, load_sem.at[4 + i])
        for i, (src, dst) in enumerate(((m1.at[0], o_m1), (m2.at[0], o_m2), (acc.at[0], o_acc), (anc, o_anc), (mom, o_mom)))
    ]
    pl.semaphore_wait(barrier, len(others))

    sends = []

    def send(src, dst, s_sem, r_sem, to):
        copy = pltpu.make_async_remote_copy(
            src_ref=src, dst_ref=dst, send_sem=s_sem, recv_sem=r_sem, device_id=to, device_id_type=MESH
        )
        copy.start()
        sends.append(copy)
        return copy

    ag = {}

    def ag_send(w, j, k, from_slot, to_slot, first, count, to):
        rows = pl.ds(j * CH + first, count)
        src = dn.at[0, rows] if w == 1 and from_slot == 0 else W.at[w, from_slot, rows]
        ag[w, j, k] = send(src, W.at[w, to_slot, rows], ags.at[w, j, k], agr.at[w, j, k], to)

    def ag_own_z(w, j):
        ag_send(w, j, 2, 0, 4, 0, CH, zp)

    def ag_own_y(w, j):
        ag_send(w, j, 0, 0, 3, 0, CH, yp)
        ag_send(w, j, 1, 0, 1, 0, CH, ym)

    def ag_half(w, j):
        ag[w, j, 0].wait_recv()
        ag_send(w, j, 5, 3, 2, 0, HALF, yp)
        if (w, j) in BY_Z_AG:
            ag_send(w, j, 8, 3, 7, HALF, HALF, zp)
        ag[w, j, 1].wait_recv()
        ag_send(w, j, 6, 1, 2, HALF, HALF, ym)
        if (w, j) in BY_Z_AG:
            ag_send(w, j, 9, 1, 5, HALF, HALF, zp)

    def ag_far(w, j):
        ag[w, j, 2].wait_recv()
        count = HALF if (w, j) in BY_Z_AG else CH
        ag_send(w, j, 3, 4, 7, 0, count, yp)
        ag_send(w, j, 4, 4, 5, 0, count, ym)

    def ag_last(w, j):
        ag[w, j, 5].wait_recv()
        ag[w, j, 6].wait_recv()
        ag_send(w, j, 7, 2, 6, 0, CH, zp)

    def ag_end(w, j):
        for k in (3, 4, 7, 8, 9) if (w, j) in BY_Z_AG else (3, 4, 7):
            ag[w, j, k].wait_recv()

    begun = set()

    def forward(w, j, slots):
        first = w not in begun
        begun.add(w)
        rows = pl.ds(j * CH, CH)

        @pl.loop(0, 4)
        def _(t):
            at = pl.ds(pl.multiple_of(t * 128, 128), 128)
            total = None if first else A[w, at]
            for s in slots:
                part = jnp.dot(X[w, s, at, rows], W[w, s, rows], preferred_element_type=jnp.float32)
                total = part if total is None else total + part
            A[w, at] = total

    def up_cast(j):
        up_load[j].wait()
        W[0, 0, chunk[j]] = U[chunk[j]].astype(jnp.bfloat16)

    x_local, x_send = [[], []], [[], []]

    def x_start():
        for w, src in enumerate((tok, cot)):
            for s in range(8):
                mine = pl.ds(pl.multiple_of(shard_at(s % 4, s // 4, c) * ROWS, ROWS), ROWS)
                its = pl.ds(pl.multiple_of(shard_at(s % 4, s // 4, 1 - c) * ROWS, ROWS), ROWS)
                copy = pltpu.make_async_copy(src.at[0, :, mine], X.at[w, s, pl.ds(0, TOK)], x_sem.at[w, s])
                copy.start()
                x_local[w].append(copy)
                x_send[w].append(
                    send(src.at[0, :, its], X.at[w, s, pl.ds(TOK, TOK)], xs_sem.at[w, s], xr_sem.at[w, s], partner)
                )
        dn_load.start()
        for copy in late:
            copy.start()

    def x_wait(w):
        for s in range(8):
            x_local[w][s].wait()
            x_send[w][s].wait_recv()
        if w == 1:
            dn_load.wait()

    near, far = (0, 1, 3, 4), (2, 5, 6, 7)
    partial, hidden = {}, {}

    def act():
        @pl.loop(0, 2)
        def _(t):
            at = pl.ds(pl.multiple_of(t * 128, 128), 128)
            v = (A[0, at] + R[0, at]) * D ** (-0.5)
            R[0, at] = v
            act = 0.5 * v * (1.0 + jnp.tanh(GELU_K * (v + GELU_C * (v * v * v))))
            G[1, 0, :, at] = act.T.astype(jnp.bfloat16)

    def grad():
        @pl.loop(0, 2)
        def _(t):
            at = pl.ds(pl.multiple_of(t * 128, 128), 128)
            upstream = (A[1, at] + R[1, at]) * FFW ** (-0.5)
            v = R[0, at]
            squared = v * v
            th = jnp.tanh(GELU_K * (v + GELU_C * (v * squared)))
            slope = 0.5 * (1.0 + th) + 0.5 * v * (1.0 - th * th) * (GELU_K * (1.0 + 3.0 * GELU_C * squared))
            G[0, 0, :, at] = (upstream * slope).T.astype(jnp.bfloat16)

    def swap_partial(w):
        partial[w] = send(A.at[w, pl.ds(TOK, TOK)], R.at[w], ps.at[w], pr.at[w], partner)

    def swap_hidden(w):
        hidden[w] = send(G.at[w, 0], G.at[w, 1], gs.at[w], gr.at[w], partner)

    def terms(w, j):
        rows = pl.ds(j * CH, CH)
        scale = D ** (-0.5) if w == 0 else FFW ** (-0.5)

        @pl.loop(0, 8)
        def _(s):
            part = jnp.dot(G[w, 0], X[w, s, pl.ds(0, TOK), rows], preferred_element_type=jnp.float32)
            part += jnp.dot(G[w, 1], X[w, s, pl.ds(TOK, TOK), rows], preferred_element_type=jnp.float32)
            T[w, j, s] = (part * scale).astype(jnp.bfloat16)

    rs = {}

    def rs_send(w, j, k, src, dst, to):
        rs[w, j, k] = send(src, dst, rss.at[w, j, k], rsr.at[w, j, k], to)

    low, high, full = pl.ds(0, HALF_F), pl.ds(HALF_F, HALF_F), pl.ds(0, FFW)

    def rs_one_z(w, j):
        rs_send(w, j, 0, T.at[w, j, 6], B.at[w, j, 0], zp)

    def rs_one_y(w, j):
        by_z = (w, j) in BY_Z_RS
        to_yp, to_ym = (low, high) if by_z else (full, full)
        rs_send(w, j, 1, T.at[w, j, 5, to_yp], B.at[w, j, 1, to_yp], yp)
        rs_send(w, j, 2, T.at[w, j, 7, to_ym], B.at[w, j, 2, to_ym], ym)
        if by_z:
            rs_send(w, j, 8, T.at[w, j, 5, high], B.at[w, j, 7, high], zp)
            rs_send(w, j, 9, T.at[w, j, 7, low], B.at[w, j, 7, low], zp)

    def add(w, j, slot, rows, *held):
        total = T[w, j, slot, rows].astype(jnp.float32)
        for k in held:
            total += B[w, j, k, rows].astype(jnp.float32)
        T[w, j, slot, rows] = total.astype(jnp.bfloat16)

    def rs_two_y(w, j):
        rs[w, j, 0].wait_recv()
        add(w, j, 2, full, 0)
        rs_send(w, j, 3, T.at[w, j, 2, low], B.at[w, j, 3, low], yp)
        rs_send(w, j, 4, T.at[w, j, 2, high], B.at[w, j, 3, high], ym)

    def rs_two_z(w, j):
        rs[w, j, 1].wait_recv()
        rs[w, j, 2].wait_recv()
        if (w, j) in BY_Z_RS:
            add(w, j, 4, low, 1)
            add(w, j, 4, high, 2)
        else:
            add(w, j, 4, full, 1, 2)
        rs_send(w, j, 5, T.at[w, j, 4], B.at[w, j, 4], zp)

    def rs_three_a(w, j):
        if (w, j) in BY_Z_RS:
            rs[w, j, 8].wait_recv()
            add(w, j, 1, high, 7)
            rs[w, j, 9].wait_recv()
            add(w, j, 3, low, 7)
        rs_send(w, j, 10, T.at[w, j, 1, high], B.at[w, j, 5, high], yp)
        rs_send(w, j, 11, T.at[w, j, 3, low], B.at[w, j, 6, low], ym)

    def rs_three_b(w, j):
        rs[w, j, 3].wait_recv()
        add(w, j, 1, low, 3)
        rs_send(w, j, 6, T.at[w, j, 1, low], B.at[w, j, 5, low], yp)
        rs[w, j, 4].wait_recv()
        add(w, j, 3, high, 3)
        rs_send(w, j, 7, T.at[w, j, 3, high], B.at[w, j, 6, high], ym)

    def rs_four(w, j):
        for k in (5, 6, 7, 10, 11):
            rs[w, j, k].wait_recv()
        total = T[w, j, 0].astype(jnp.float32)
        for k in (4, 5, 6):
            total += B[w, j, k].astype(jnp.float32)
        return total.T

    ar = {}

    def adam(j):
        rows = pl.ds(j * CH, CH)
        grad = rs_four(0, j)
        first = beta_one * o_m1[rows] + (1.0 - beta_one) * grad
        o_m1[rows] = first
        second = beta_two * o_m2[rows] + (1.0 - beta_two) * grad * grad
        o_m2[rows] = second
        master = U[rows]
        stepped = master - inner_rate * (
            first / fix_one / (jnp.sqrt(second / fix_two) + adam_eps) + decay_rate * master
        )
        PS[j] = (o_anc[rows] - stepped).astype(jnp.bfloat16)
        for p in range(1, N_X):
            piece = pl.ds(pl.multiple_of(((x + p) % N_X) * PIECE, PIECE), PIECE)
            ar[j, p] = send(PS.at[j, piece], PR.at[j, N_X - p], ars.at[j, p], arr.at[j, N_X - p], beside[p])

    mean = {}

    def sum_x(j):
        for p in range(1, N_X):
            ar[j, p].wait_recv()
        total = PS[j, pl.ds(pl.multiple_of(x * PIECE, PIECE), PIECE)].astype(jnp.float32)
        for p in range(1, N_X):
            total += PR[j, p].astype(jnp.float32)
        PR[j, 0] = total.astype(jnp.bfloat16)
        ar[j, 0] = send(PR.at[j, 0], PR.at[j, N_X], ars.at[j, 0], arr.at[j, 0], above)

    def sum_z(j):
        ar[j, 0].wait_recv()
        mine = pl.ds(pl.multiple_of(x * PIECE, PIECE), PIECE)
        total = PR[j, 0].astype(jnp.float32) + PR[j, N_X].astype(jnp.float32)
        MN[j, mine] = (total / N_REP).astype(jnp.bfloat16)
        for p in range(1, N_X):
            mean[j, p] = send(MN.at[j, mine], MN.at[j, mine], mns.at[j, p], mnr.at[j, N_X - p], beside[p])

    def outer(j):
        rows = pl.ds(j * CH, CH)
        for p in range(1, N_X):
            mean[j, p].wait_recv()
        outer_mean = MN[j].astype(jnp.float32)
        new_momentum = outer_mu * o_mom[rows] + outer_mean
        o_mom[rows] = new_momentum
        o_anc[rows] = o_anc[rows] - outer_rate * (outer_mean + outer_mu * new_momentum)

    def down(j):
        rows = pl.ds(j * CH, CH)
        o_acc[rows] = o_acc[rows] + rs_four(1, j)

    ag_own_z(1, 2)
    ag_own_y(1, 1)
    up_cast(2)
    up_cast(1)
    up_cast(0)
    ag_own_y(0, 0)
    ag_own_z(0, 2)
    ag_own_z(0, 1)
    ag_own_y(0, 1)
    x_start()
    ag_own_z(0, 0)
    ag_own_y(0, 2)
    ag_own_y(1, 0)
    ag_far(0, 1)
    ag_half(0, 0)
    x_wait(0)
    ag_half(0, 1)
    ag_own_y(1, 2)
    ag_half(0, 2)
    ag_half(1, 0)
    ag_own_z(1, 0)
    forward(0, 1, near)
    ag_far(0, 0)
    ag_last(0, 0)
    ag_last(0, 1)
    ag_last(0, 2)
    ag_own_z(1, 1)
    ag_far(0, 2)
    ag_half(1, 1)
    ag_last(1, 0)
    forward(0, 0, near)
    ag_end(0, 1)
    forward(0, 1, far)
    ag_far(1, 0)
    forward(0, 2, near)
    ag_end(0, 0)
    forward(0, 0, far)
    ag_end(0, 2)
    ag_half(1, 2)
    forward(0, 2, far)
    x_wait(1)
    swap_partial(0)
    ag_last(1, 1)
    forward(1, 0, near)
    partial[0].wait_recv()
    act()
    swap_hidden(1)
    ag_far(1, 1)
    forward(1, 1, near)
    hidden[1].wait_recv()
    terms(1, 1)
    ag_last(1, 2)
    ag_far(1, 2)
    ag_end(1, 0)
    forward(1, 2, near)
    rs_one_z(1, 1)
    terms(1, 0)
    ag_end(1, 1)
    rs_one_z(1, 0)
    rs_three_a(1, 1)
    rs_one_y(1, 0)
    forward(1, 1, far)
    forward(1, 0, far)
    ag_end(1, 2)
    forward(1, 2, far)
    swap_partial(1)
    rs_one_y(1, 1)
    partial[1].wait_recv()
    grad()
    swap_hidden(0)
    hidden[0].wait_recv()
    terms(0, 2)
    rs_one_y(0, 2)
    rs_three_a(0, 2)
    rs_one_z(0, 2)
    terms(0, 1)
    rs_one_z(0, 1)
    terms(0, 0)
    rs_one_y(0, 1)
    rs_one_z(0, 0)
    rs_two_y(0, 2)
    rs_one_y(0, 0)
    rs_two_z(0, 2)
    rs_two_y(0, 1)
    rs_two_y(0, 0)
    rs_three_b(0, 2)
    terms(1, 2)
    rs_three_b(0, 1)
    rs_three_a(0, 1)
    rs_two_z(0, 1)
    rs_three_a(0, 0)
    rs_two_z(0, 0)
    rs_one_z(1, 2)
    rs_three_b(0, 0)
    rs_two_y(1, 1)
    rs_two_z(1, 1)
    rs_one_y(1, 2)
    rs_two_y(1, 0)
    rs_three_a(1, 0)
    for copy in late:
        copy.wait()
    adam(2)
    adam(1)
    adam(0)
    rs_two_z(1, 0)
    sum_x(2)
    sum_x(1)
    rs_two_y(1, 2)
    rs_two_z(1, 2)
    rs_three_b(1, 1)
    rs_three_b(1, 0)
    sum_x(0)
    sum_z(2)
    rs_three_b(1, 2)
    sum_z(1)
    rs_three_a(1, 2)
    down(1)
    sum_z(0)
    down(0)
    outer(2)
    outer(1)
    down(2)
    outer(0)
    for copy in sends:
        copy.wait_send()


def place(anc, mom, m1, m2, acc, o_anc, o_mom, o_m1, o_m2, o_acc, sem):
    pairs = ((anc, o_anc), (mom, o_mom), (m1, o_m1.at[0]), (m2, o_m2.at[0]), (acc, o_acc.at[0]))
    copies = [pltpu.make_async_copy(src, dst, sem.at[i]) for i, (src, dst) in enumerate(pairs)]
    for copy in copies:
        copy.start()
    for copy in copies:
        copy.wait()


def on_device(tokens, cotangent, inner_up, adam_first, adam_second, inner_down, down_accum, anchor_up, outer_momentum):
    flat = jax.ShapeDtypeStruct((ROWS, FFW), jnp.float32)
    deep = jax.ShapeDtypeStruct((1, ROWS, FFW), jnp.float32)
    dma = pltpu.SemaphoreType.DMA
    bf16, f32 = jnp.bfloat16, jnp.float32
    held = pl.pallas_call(
        kernel,
        out_shape=(pltpu.VMEM((ROWS, FFW), f32),) * 5,
        in_specs=[pl.BlockSpec(memory_space=pl.ANY)] * 9,
        out_specs=[pl.BlockSpec(memory_space=pltpu.VMEM)] * 5,
        scratch_shapes=[
            pltpu.VMEM((2, 8, 2 * TOK, ROWS), bf16),
            pltpu.VMEM((2, 8, ROWS, FFW), bf16),
            pltpu.VMEM((2, 2 * TOK, FFW), f32),
            pltpu.VMEM((2, TOK, FFW), f32),
            pltpu.VMEM((2, 2, FFW, TOK), bf16),
            pltpu.VMEM((2, NCH, 8, FFW, CH), bf16),
            pltpu.VMEM((2, NCH, 8, FFW, CH), bf16),
            pltpu.VMEM((ROWS, FFW), f32),
            pltpu.VMEM((NCH, CH, FFW), bf16),
            pltpu.VMEM((NCH, N_X + 1, PIECE, FFW), bf16),
            pltpu.VMEM((NCH, CH, FFW), bf16),
            dma((9,)),
            dma((2, 8)),
            dma((2, 8)),
            dma((2, 8)),
            dma((2, NCH, 10)),
            dma((2, NCH, 10)),
            dma((2, NCH, 12)),
            dma((2, NCH, 12)),
            dma((2,)),
            dma((2,)),
            dma((2,)),
            dma((2,)),
            dma((NCH, N_X)),
            dma((NCH, N_X)),
            dma((NCH, N_X)),
            dma((NCH, N_X)),
        ],
        name="window",
        compiler_params=pltpu.CompilerParams(
            collective_id=0, has_side_effects=True, vmem_limit_bytes=52 * 2**20
        ),
        cost_estimate=pl.CostEstimate(flops=9_700_000_000, bytes_accessed=30_000_000, transcendentals=200_000),
    )(tokens, cotangent, inner_up, adam_first, adam_second, inner_down, down_accum, anchor_up, outer_momentum)
    return pl.pallas_call(
        place,
        out_shape=(flat, flat, deep, deep, deep),
        in_specs=[pl.BlockSpec(memory_space=pltpu.VMEM)] * 5,
        out_specs=[pl.BlockSpec(memory_space=pl.ANY)] * 5,
        scratch_shapes=[dma((5,))],
        name="place",
        compiler_params=pltpu.CompilerParams(vmem_limit_bytes=2**20),
    )(*(pltpu.with_memory_space_constraint(value, pltpu.VMEM) for value in held))


def solution(mesh):
    return jax.shard_map(
        on_device,
        mesh=mesh,
        in_specs=(
            P("replica", "shard", None),
            P("replica", "shard", None),
            P("replica", "shard", None),
            P("replica", "shard", None),
            P("replica", "shard", None),
            P("replica", "shard", None),
            P("replica", "shard", None),
            P("shard", None),
            P("shard", None),
        ),
        out_specs=(
            P("shard", None),
            P("shard", None),
            P("replica", "shard", None),
            P("replica", "shard", None),
            P("replica", "shard", None),
        ),
        check_vma=False,
    )
```

```python
import jax
import jax.numpy as jnp
from jax import lax
from jax.experimental import pallas as pl
from jax.experimental.pallas import tpu as pltpu
from jax.sharding import PartitionSpec as P

MESH = pl.DeviceIdType.MESH
D = 12288
FFW = 384
TOK = 256
ROWS = 768
CH = 256
NCH = 3
LAST = 2
HALF = CH // 2
HALF_F = FFW // 2
N_REP = 8
N_X = 4
PIECE = CH // N_X
AG_Z = {(0, 1): 128, (0, 2): 128}
RS_Z = {(0, 0): 192}

beta_one = 0.8
beta_two = 0.95
inner_rate = 0.05
decay_rate = 0.1
adam_eps = 1e-08
adam_steps = 20
outer_mu = 0.9
outer_rate = 0.7
fix_one = 1.0 - beta_one**adam_steps
fix_two = 1.0 - beta_two**adam_steps
GELU_K = 0.7978845608028654
GELU_C = 0.044715


def kernel(
    tok, cot, up, m1, m2, dn, acc, anc, mom,
    o_anc, o_mom, o_m1, o_m2, o_acc, E,
    X, W, A, R, G, T, B, U, PS, PR, MN,
    load_sem, x_sem, xs_sem, xr_sem, ags, agr, rss, rsr, ps, pr, gs, gr, ars, arr, mns, mnr,
):
    rep = lax.axis_index("replica")
    shd = lax.axis_index("shard")
    x, zl = rep % 4, rep // 4
    c, y, zh = shd % 2, (shd // 2) % 4, shd // 8

    def shard_at(dy, dz, core):
        return ((zh + dz) % 2) * 8 + ((y + dy) % 4) * 2 + core

    partner = (rep, shard_at(0, 0, 1 - c))
    yp = (rep, shard_at(1, 0, c))
    ym = (rep, shard_at(3, 0, c))
    zp = (rep, shard_at(0, 1, c))

    beside = [(zl * 4 + (x + p) % 4, shd) for p in range(4)]
    above = ((1 - zl) * 4 + x, shd)

    barrier = pltpu.get_barrier_semaphore()
    others = [partner, yp, ym, zp, above] + beside[1:]
    for other in others:
        pl.semaphore_signal(barrier, inc=1, device_id=other, device_id_type=MESH)

    chunk = [pl.ds(j * CH, CH) for j in range(NCH)]
    up_load = [pltpu.make_async_copy(up.at[0, chunk[j]], U.at[chunk[j]], load_sem.at[j]) for j in range(NCH)]
    for copy in up_load:
        copy.start()
    dn_load = pltpu.make_async_copy(dn.at[0], W.at[1, 0], load_sem.at[3])
    late = [
        pltpu.make_async_copy(src, dst, load_sem.at[4 + i])
        for i, (src, dst) in enumerate(((m1.at[0], o_m1), (m2.at[0], o_m2), (acc.at[0], o_acc), (anc, o_anc), (mom, o_mom)))
    ]
    pl.semaphore_wait(barrier, len(others))

    sends = []

    def send(src, dst, s_sem, r_sem, to):
        copy = pltpu.make_async_remote_copy(
            src_ref=src, dst_ref=dst, send_sem=s_sem, recv_sem=r_sem, device_id=to, device_id_type=MESH
        )
        copy.start()
        sends.append(copy)
        return copy

    ag = {}

    def ag_send(w, j, k, from_slot, to_slot, first, count, to):
        rows = pl.ds(j * CH + first, count)
        src = dn.at[0, rows] if w == 1 and from_slot == 0 else W.at[w, from_slot, rows]
        ag[w, j, k] = send(src, W.at[w, to_slot, rows], ags.at[w, j, k], agr.at[w, j, k], to)

    def ag_own_z(w, j):
        ag_send(w, j, 2, 0, 4, 0, CH, zp)

    def ag_own_y(w, j):
        ag_send(w, j, 0, 0, 3, 0, CH, yp)
        ag_send(w, j, 1, 0, 1, 0, CH, ym)

    def ag_half(w, j):
        by_z = AG_Z.get((w, j), 0)
        ag[w, j, 0].wait_recv()
        ag_send(w, j, 5, 3, 2, 0, HALF, yp)
        if by_z:
            ag_send(w, j, 8, 3, 7, CH - by_z, by_z, zp)
        ag[w, j, 1].wait_recv()
        ag_send(w, j, 6, 1, 2, HALF, HALF, ym)
        if by_z:
            ag_send(w, j, 9, 1, 5, CH - by_z, by_z, zp)

    def ag_far(w, j):
        ag[w, j, 2].wait_recv()
        count = CH - AG_Z.get((w, j), 0)
        ag_send(w, j, 3, 4, 7, 0, count, yp)
        ag_send(w, j, 4, 4, 5, 0, count, ym)

    def ag_last(w, j):
        ag[w, j, 5].wait_recv()
        ag[w, j, 6].wait_recv()
        ag_send(w, j, 7, 2, 6, 0, CH, zp)

    def ag_end(w, j):
        for k in (3, 4, 7, 8, 9) if AG_Z.get((w, j)) else (3, 4, 7):
            ag[w, j, k].wait_recv()

    begun = set()

    def forward(w, j, slots):
        first = w not in begun
        begun.add(w)
        rows = pl.ds(j * CH, CH)

        @pl.loop(0, 4)
        def _(t):
            at = pl.ds(pl.multiple_of(t * 128, 128), 128)
            total = None if first else A[w, at]
            for s in slots:
                part = jnp.dot(X[w, s, at, rows], W[w, s, rows], preferred_element_type=jnp.float32)
                total = part if total is None else total + part
            A[w, at] = total

    def up_cast(j):
        up_load[j].wait()
        W[0, 0, chunk[j]] = U[chunk[j]].astype(jnp.bfloat16)

    x_local, x_send = [[], []], [[], []]

    def x_start():
        for w, src in enumerate((tok, cot)):
            for s in range(8):
                mine = pl.ds(pl.multiple_of(shard_at(s % 4, s // 4, c) * ROWS, ROWS), ROWS)
                its = pl.ds(pl.multiple_of(shard_at(s % 4, s // 4, 1 - c) * ROWS, ROWS), ROWS)
                copy = pltpu.make_async_copy(src.at[0, :, mine], X.at[w, s, pl.ds(0, TOK)], x_sem.at[w, s])
                copy.start()
                x_local[w].append(copy)
                x_send[w].append(
                    send(src.at[0, :, its], X.at[w, s, pl.ds(TOK, TOK)], xs_sem.at[w, s], xr_sem.at[w, s], partner)
                )
        dn_load.start()
        for copy in late:
            copy.start()

    def x_wait(w):
        for s in range(8):
            x_local[w][s].wait()
            x_send[w][s].wait_recv()
        if w == 1:
            dn_load.wait()

    near, far = (0, 1, 3, 4), (2, 5, 6, 7)
    partial, hidden = {}, {}

    def act():
        @pl.loop(0, 2)
        def _(t):
            at = pl.ds(pl.multiple_of(t * 128, 128), 128)
            v = (A[0, at] + R[0, at]) * D ** (-0.5)
            R[0, at] = v
            act = 0.5 * v * (1.0 + jnp.tanh(GELU_K * (v + GELU_C * (v * v * v))))
            G[1, 0, :, at] = act.T.astype(jnp.bfloat16)

    def grad():
        @pl.loop(0, 2)
        def _(t):
            at = pl.ds(pl.multiple_of(t * 128, 128), 128)
            upstream = (A[1, at] + R[1, at]) * FFW ** (-0.5)
            v = R[0, at]
            squared = v * v
            th = jnp.tanh(GELU_K * (v + GELU_C * (v * squared)))
            slope = 0.5 * (1.0 + th) + 0.5 * v * (1.0 - th * th) * (GELU_K * (1.0 + 3.0 * GELU_C * squared))
            G[0, 0, :, at] = (upstream * slope).T.astype(jnp.bfloat16)

    def swap_partial(w):
        partial[w] = send(A.at[w, pl.ds(TOK, TOK)], R.at[w], ps.at[w], pr.at[w], partner)

    def swap_hidden(w):
        hidden[w] = send(G.at[w, 0], G.at[w, 1], gs.at[w], gr.at[w], partner)

    def terms(w, j):
        rows = pl.ds(j * CH, CH)
        scale = D ** (-0.5) if w == 0 else FFW ** (-0.5)

        @pl.loop(0, 8)
        def _(s):
            part = jnp.dot(G[w, 0], X[w, s, pl.ds(0, TOK), rows], preferred_element_type=jnp.float32)
            part += jnp.dot(G[w, 1], X[w, s, pl.ds(TOK, TOK), rows], preferred_element_type=jnp.float32)
            T[w, j, s] = (part * scale).astype(jnp.bfloat16)

        if (w, j) == (1, LAST):
            E[3] = T[w, j, 0]

    rs = {}

    def rs_send(w, j, k, src, dst, to):
        rs[w, j, k] = send(src, dst, rss.at[w, j, k], rsr.at[w, j, k], to)

    low, high, full = pl.ds(0, HALF_F), pl.ds(HALF_F, HALF_F), pl.ds(0, FFW)

    def home(w, j, k):
        return E.at[k - 4] if (w, j) == (1, LAST) else B.at[w, j, k]

    def rs_one_z(w, j):
        rs_send(w, j, 0, T.at[w, j, 6], B.at[w, j, 0], zp)

    def rs_one_y(w, j):
        by_z = RS_Z.get((w, j), 0)
        to_yp, to_ym = pl.ds(0, FFW - by_z), pl.ds(by_z, FFW - by_z)
        rs_send(w, j, 1, T.at[w, j, 5, to_yp], B.at[w, j, 1, to_yp], yp)
        rs_send(w, j, 2, T.at[w, j, 7, to_ym], B.at[w, j, 2, to_ym], ym)
        if by_z:
            first, last = pl.ds(0, by_z), pl.ds(FFW - by_z, by_z)
            rs_send(w, j, 8, T.at[w, j, 5, last], B.at[w, j, 7, last], zp)
            rs_send(w, j, 9, T.at[w, j, 7, first], B.at[w, j, 7, first], zp)

    def add(w, j, slot, rows, *held):
        total = T[w, j, slot, rows].astype(jnp.float32)
        for k in held:
            total += B[w, j, k, rows].astype(jnp.float32)
        T[w, j, slot, rows] = total.astype(jnp.bfloat16)

    def rs_two_y(w, j):
        rs[w, j, 0].wait_recv()
        add(w, j, 2, full, 0)
        rs_send(w, j, 3, T.at[w, j, 2, low], B.at[w, j, 3, low], yp)
        rs_send(w, j, 4, T.at[w, j, 2, high], B.at[w, j, 3, high], ym)

    def rs_two_z(w, j):
        by_z = RS_Z.get((w, j), 0)
        rs[w, j, 1].wait_recv()
        rs[w, j, 2].wait_recv()
        if by_z:
            add(w, j, 4, pl.ds(0, by_z), 1)
            add(w, j, 4, pl.ds(FFW - by_z, by_z), 2)
        if by_z < HALF_F:
            add(w, j, 4, pl.ds(by_z, FFW - 2 * by_z), 1, 2)
        rs_send(w, j, 5, T.at[w, j, 4], home(w, j, 4), zp)

    def rs_three_a(w, j):
        by_z = RS_Z.get((w, j), 0)
        if by_z:
            rs[w, j, 8].wait_recv()
            add(w, j, 1, pl.ds(FFW - by_z, by_z), 7)
            rs[w, j, 9].wait_recv()
            add(w, j, 3, pl.ds(0, by_z), 7)
        rs_send(w, j, 10, T.at[w, j, 1, high], home(w, j, 5).at[high], yp)
        rs_send(w, j, 11, T.at[w, j, 3, low], home(w, j, 6).at[low], ym)

    def rs_three_b(w, j):
        rs[w, j, 3].wait_recv()
        add(w, j, 1, low, 3)
        rs_send(w, j, 6, T.at[w, j, 1, low], home(w, j, 5).at[low], yp)
        rs[w, j, 4].wait_recv()
        add(w, j, 3, high, 3)
        rs_send(w, j, 7, T.at[w, j, 3, high], home(w, j, 6).at[high], ym)

    def rs_four(w, j):
        for k in (5, 6, 7, 10, 11):
            rs[w, j, k].wait_recv()
        total = T[w, j, 0].astype(jnp.float32)
        for k in (4, 5, 6):
            total += B[w, j, k].astype(jnp.float32)
        return total.T

    ar = {}

    def adam(j):
        rows = pl.ds(j * CH, CH)
        grad = rs_four(0, j)
        first = beta_one * o_m1[rows] + (1.0 - beta_one) * grad
        o_m1[rows] = first
        second = beta_two * o_m2[rows] + (1.0 - beta_two) * grad * grad
        o_m2[rows] = second
        master = U[rows]
        stepped = master - inner_rate * (
            first / fix_one / (jnp.sqrt(second / fix_two) + adam_eps) + decay_rate * master
        )
        PS[j] = (o_anc[rows] - stepped).astype(jnp.bfloat16)
        for p in range(1, N_X):
            piece = pl.ds(pl.multiple_of(((x + p) % N_X) * PIECE, PIECE), PIECE)
            ar[j, p] = send(PS.at[j, piece], PR.at[j, N_X - p], ars.at[j, p], arr.at[j, N_X - p], beside[p])

    mean = {}

    def sum_x(j):
        for p in range(1, N_X):
            ar[j, p].wait_recv()
        total = PS[j, pl.ds(pl.multiple_of(x * PIECE, PIECE), PIECE)].astype(jnp.float32)
        for p in range(1, N_X):
            total += PR[j, p].astype(jnp.float32)
        PR[j, 0] = total.astype(jnp.bfloat16)
        ar[j, 0] = send(PR.at[j, 0], PR.at[j, N_X], ars.at[j, 0], arr.at[j, 0], above)

    def sum_z(j):
        ar[j, 0].wait_recv()
        mine = pl.ds(pl.multiple_of(x * PIECE, PIECE), PIECE)
        total = PR[j, 0].astype(jnp.float32) + PR[j, N_X].astype(jnp.float32)
        MN[j, mine] = (total / N_REP).astype(jnp.bfloat16)
        for p in range(1, N_X):
            mean[j, p] = send(MN.at[j, mine], MN.at[j, mine], mns.at[j, p], mnr.at[j, N_X - p], beside[p])

    def outer(j):
        rows = pl.ds(j * CH, CH)
        for p in range(1, N_X):
            mean[j, p].wait_recv()
        outer_mean = MN[j].astype(jnp.float32)
        new_momentum = outer_mu * o_mom[rows] + outer_mean
        o_mom[rows] = new_momentum
        o_anc[rows] = o_anc[rows] - outer_rate * (outer_mean + outer_mu * new_momentum)

    def tail(j):
        for k in (5, 6, 7, 10, 11):
            rs[1, j, k].wait_recv()

    def down(j):
        rows = pl.ds(j * CH, CH)
        o_acc[rows] = o_acc[rows] + rs_four(1, j)

    ag_own_y(1, 1)
    ag_own_z(1, 1)
    up_cast(1)
    ag_own_y(0, 1)
    up_cast(0)
    ag_own_z(0, 1)
    up_cast(2)
    x_start()
    ag_own_z(0, 2)
    ag_own_y(0, 0)
    ag_half(0, 1)
    ag_far(0, 1)
    ag_own_z(1, 0)
    ag_own_y(0, 2)
    ag_half(1, 1)
    ag_own_z(0, 0)
    ag_last(0, 1)
    ag_own_y(1, 0)
    ag_half(0, 0)
    ag_half(0, 2)
    ag_far(0, 0)
    ag_end(0, 1)
    x_wait(0)
    ag_half(1, 0)
    ag_own_y(1, 2)
    ag_last(0, 0)
    forward(0, 1, far)
    ag_far(0, 2)
    forward(0, 0, near)
    ag_far(1, 0)
    x_wait(1)
    forward(1, 0, near)
    forward(0, 1, near)
    ag_last(0, 2)
    ag_last(1, 0)
    ag_half(1, 2)
    ag_far(1, 1)
    forward(1, 1, near)
    ag_own_z(1, 2)
    forward(0, 2, near)
    ag_end(0, 0)
    ag_end(0, 2)
    ag_last(1, 1)
    forward(0, 2, far)
    forward(0, 0, far)
    swap_partial(0)
    partial[0].wait_recv()
    ag_end(1, 0)
    act()
    swap_hidden(1)
    ag_last(1, 2)
    forward(1, 0, far)
    hidden[1].wait_recv()
    ag_far(1, 2)
    forward(1, 2, near)
    terms(1, 0)
    terms(1, 1)
    rs_three_a(1, 1)
    rs_one_z(1, 0)
    ag_end(1, 1)
    forward(1, 1, far)
    rs_one_y(1, 1)
    rs_one_z(1, 1)
    rs_one_y(1, 0)
    ag_end(1, 2)
    forward(1, 2, far)
    swap_partial(1)
    partial[1].wait_recv()
    grad()
    swap_hidden(0)
    hidden[0].wait_recv()
    terms(0, 2)
    rs_one_z(0, 2)
    rs_one_y(0, 2)
    terms(0, 1)
    rs_one_y(0, 1)
    rs_one_z(0, 1)
    terms(0, 0)
    rs_three_a(0, 2)
    rs_one_z(0, 0)
    rs_two_z(0, 2)
    terms(1, 2)
    rs_two_y(0, 2)
    rs_one_y(0, 0)
    rs_two_y(0, 1)
    rs_three_b(0, 2)
    rs_two_y(0, 0)
    rs_three_b(0, 1)
    rs_two_z(0, 1)
    rs_two_z(0, 0)
    rs_three_a(0, 1)
    for copy in late:
        copy.wait()
    adam(2)
    rs_three_a(0, 0)
    rs_three_b(0, 0)
    rs_one_z(1, 2)
    rs_two_z(1, 0)
    rs_two_y(1, 0)
    rs_one_y(1, 2)
    adam(1)
    sum_x(2)
    adam(0)
    rs_three_b(1, 0)
    rs_two_y(1, 1)
    sum_x(1)
    sum_z(2)
    rs_three_a(1, 0)
    rs_two_z(1, 1)
    rs_two_y(1, 2)
    sum_x(0)
    rs_three_a(1, 2)
    rs_two_z(1, 2)
    sum_z(1)
    rs_three_b(1, 1)
    sum_z(0)
    rs_three_b(1, 2)
    outer(2)
    down(0)
    outer(1)
    down(1)
    outer(0)
    tail(2)
    for copy in sends:
        copy.wait_send()


def place(anc, mom, m1, m2, acc, E, o_anc, o_mom, o_m1, o_m2, o_acc, S, sem):
    pairs = ((m1, o_m1.at[0]), (m2, o_m2.at[0]), (acc, o_acc.at[0]), (anc, o_anc), (mom, o_mom))
    chunk = [pl.ds(j * CH, CH) for j in range(NCH)]
    copies = [
        pltpu.make_async_copy(src.at[chunk[j]], dst.at[chunk[j]], sem.at[i, j])
        for i, (src, dst) in enumerate(pairs)
        for j in range(NCH)
        if (i, j) != (2, LAST)
    ]
    for copy in copies:
        copy.start()
    total = E[3].astype(jnp.float32)
    for k in range(3):
        total += E[k].astype(jnp.float32)
    S[...] = acc[chunk[LAST]] + total.T
    copies.append(pltpu.make_async_copy(S, o_acc.at[0, chunk[LAST]], sem.at[2, LAST]))
    copies[-1].start()
    for copy in copies:
        copy.wait()


def on_device(tokens, cotangent, inner_up, adam_first, adam_second, inner_down, down_accum, anchor_up, outer_momentum):
    flat = jax.ShapeDtypeStruct((ROWS, FFW), jnp.float32)
    deep = jax.ShapeDtypeStruct((1, ROWS, FFW), jnp.float32)
    dma = pltpu.SemaphoreType.DMA
    bf16, f32 = jnp.bfloat16, jnp.float32
    held = pl.pallas_call(
        kernel,
        out_shape=(pltpu.VMEM((ROWS, FFW), f32),) * 5 + (pltpu.VMEM((4, FFW, CH), bf16),),
        in_specs=[pl.BlockSpec(memory_space=pl.ANY)] * 9,
        out_specs=[pl.BlockSpec(memory_space=pltpu.VMEM)] * 6,
        scratch_shapes=[
            pltpu.VMEM((2, 8, 2 * TOK, ROWS), bf16),
            pltpu.VMEM((2, 8, ROWS, FFW), bf16),
            pltpu.VMEM((2, 2 * TOK, FFW), f32),
            pltpu.VMEM((2, TOK, FFW), f32),
            pltpu.VMEM((2, 2, FFW, TOK), bf16),
            pltpu.VMEM((2, NCH, 8, FFW, CH), bf16),
            pltpu.VMEM((2, NCH, 8, FFW, CH), bf16),
            pltpu.VMEM((ROWS, FFW), f32),
            pltpu.VMEM((NCH, CH, FFW), bf16),
            pltpu.VMEM((NCH, N_X + 1, PIECE, FFW), bf16),
            pltpu.VMEM((NCH, CH, FFW), bf16),
            dma((9,)),
            dma((2, 8)),
            dma((2, 8)),
            dma((2, 8)),
            dma((2, NCH, 10)),
            dma((2, NCH, 10)),
            dma((2, NCH, 12)),
            dma((2, NCH, 12)),
            dma((2,)),
            dma((2,)),
            dma((2,)),
            dma((2,)),
            dma((NCH, N_X)),
            dma((NCH, N_X)),
            dma((NCH, N_X)),
            dma((NCH, N_X)),
        ],
        name="window",
        compiler_params=pltpu.CompilerParams(
            collective_id=0, has_side_effects=True, vmem_limit_bytes=50 * 2**20
        ),
        cost_estimate=pl.CostEstimate(flops=9_700_000_000, bytes_accessed=30_000_000, transcendentals=200_000),
    )(tokens, cotangent, inner_up, adam_first, adam_second, inner_down, down_accum, anchor_up, outer_momentum)
    return pl.pallas_call(
        place,
        out_shape=(flat, flat, deep, deep, deep),
        in_specs=[pl.BlockSpec(memory_space=pltpu.VMEM)] * 6,
        out_specs=[pl.BlockSpec(memory_space=pl.ANY)] * 5,
        scratch_shapes=[pltpu.VMEM((CH, FFW), f32), dma((5, NCH))],
        name="place",
        compiler_params=pltpu.CompilerParams(vmem_limit_bytes=4 * 2**20),
    )(*(pltpu.with_memory_space_constraint(value, pltpu.VMEM) for value in held))


def solution(mesh):
    return jax.shard_map(
        on_device,
        mesh=mesh,
        in_specs=(
            P("replica", "shard", None),
            P("replica", "shard", None),
            P("replica", "shard", None),
            P("replica", "shard", None),
            P("replica", "shard", None),
            P("replica", "shard", None),
            P("replica", "shard", None),
            P("shard", None),
            P("shard", None),
        ),
        out_specs=(
            P("shard", None),
            P("shard", None),
            P("replica", "shard", None),
            P("replica", "shard", None),
            P("replica", "shard", None),
        ),
        check_vma=False,
    )
```

```python
import jax
import jax.numpy as jnp
from jax import lax
from jax.experimental import pallas as pl
from jax.experimental.pallas import tpu as pltpu
from jax.sharding import PartitionSpec as P

MESH = pl.DeviceIdType.MESH
D = 12288
FFW = 384
TOK = 256
ROWS = 768
CH = 256
NCH = 3
LAST = 2
HALF = CH // 2
HALF_F = FFW // 2
N_REP = 8
N_X = 4
PIECE = CH // N_X
AG_Z = {(0, 1): 128, (0, 2): 128}
RS_Z = {(0, 0): 192}

beta_one = 0.8
beta_two = 0.95
inner_rate = 0.05
decay_rate = 0.1
adam_eps = 1e-08
adam_steps = 20
outer_mu = 0.9
outer_rate = 0.7
fix_one = 1.0 - beta_one**adam_steps
fix_two = 1.0 - beta_two**adam_steps
GELU_K = 0.7978845608028654
GELU_C = 0.044715


def kernel(
    tok, cot, up, m1, m2, dn, acc, anc, mom,
    o_anc, o_mom, o_m1, o_m2, o_acc, E,
    X, W, A, R, G, T, B, U, PS, PR, MN,
    load_sem, x_sem, xs_sem, xr_sem, ags, agr, rss, rsr, ps, pr, gs, gr, ars, arr, mns, mnr,
):
    rep = lax.axis_index("replica")
    shd = lax.axis_index("shard")
    x, zl = rep % 4, rep // 4
    c, y, zh = shd % 2, (shd // 2) % 4, shd // 8

    def shard_at(dy, dz, core):
        return ((zh + dz) % 2) * 8 + ((y + dy) % 4) * 2 + core

    partner = (rep, shard_at(0, 0, 1 - c))
    yp = (rep, shard_at(1, 0, c))
    ym = (rep, shard_at(3, 0, c))
    zp = (rep, shard_at(0, 1, c))

    beside = [(zl * 4 + (x + p) % 4, shd) for p in range(4)]
    above = ((1 - zl) * 4 + x, shd)

    barrier = pltpu.get_barrier_semaphore()
    others = [partner, yp, ym, zp, above] + beside[1:]
    for other in others:
        pl.semaphore_signal(barrier, inc=1, device_id=other, device_id_type=MESH)

    chunk = [pl.ds(j * CH, CH) for j in range(NCH)]
    up_load = [pltpu.make_async_copy(up.at[0, chunk[j]], U.at[chunk[j]], load_sem.at[j]) for j in range(NCH)]
    for copy in up_load:
        copy.start()
    dn_load = pltpu.make_async_copy(dn.at[0], W.at[1, 0], load_sem.at[3])
    late = [
        pltpu.make_async_copy(src, dst, load_sem.at[4 + i])
        for i, (src, dst) in enumerate(((m1.at[0], o_m1), (m2.at[0], o_m2), (acc.at[0], o_acc), (anc, o_anc), (mom, o_mom)))
    ]
    pl.semaphore_wait(barrier, len(others))

    sends = []

    def send(src, dst, s_sem, r_sem, to):
        copy = pltpu.make_async_remote_copy(
            src_ref=src, dst_ref=dst, send_sem=s_sem, recv_sem=r_sem, device_id=to, device_id_type=MESH
        )
        copy.start()
        sends.append(copy)
        return copy

    ag = {}

    def ag_send(w, j, k, from_slot, to_slot, first, count, to):
        rows = pl.ds(j * CH + first, count)
        src = dn.at[0, rows] if w == 1 and from_slot == 0 else W.at[w, from_slot, rows]
        ag[w, j, k] = send(src, W.at[w, to_slot, rows], ags.at[w, j, k], agr.at[w, j, k], to)

    def ag_own_z(w, j):
        ag_send(w, j, 2, 0, 4, 0, CH, zp)

    def ag_own_y(w, j):
        ag_send(w, j, 0, 0, 3, 0, CH, yp)
        ag_send(w, j, 1, 0, 1, 0, CH, ym)

    def ag_half(w, j):
        by_z = AG_Z.get((w, j), 0)
        ag[w, j, 0].wait_recv()
        ag_send(w, j, 5, 3, 2, 0, HALF, yp)
        if by_z:
            ag_send(w, j, 8, 3, 7, CH - by_z, by_z, zp)
        ag[w, j, 1].wait_recv()
        ag_send(w, j, 6, 1, 2, HALF, HALF, ym)
        if by_z:
            ag_send(w, j, 9, 1, 5, CH - by_z, by_z, zp)

    def ag_far(w, j):
        ag[w, j, 2].wait_recv()
        count = CH - AG_Z.get((w, j), 0)
        ag_send(w, j, 3, 4, 7, 0, count, yp)
        ag_send(w, j, 4, 4, 5, 0, count, ym)

    def ag_last(w, j):
        ag[w, j, 5].wait_recv()
        ag[w, j, 6].wait_recv()
        ag_send(w, j, 7, 2, 6, 0, CH, zp)

    def ag_end(w, j):
        for k in (3, 4, 7, 8, 9) if AG_Z.get((w, j)) else (3, 4, 7):
            ag[w, j, k].wait_recv()

    begun = set()

    def forward(w, j, slots):
        first = w not in begun
        begun.add(w)
        rows = pl.ds(j * CH, CH)

        @pl.loop(0, 4)
        def _(t):
            at = pl.ds(pl.multiple_of(t * 128, 128), 128)
            total = None if first else A[w, at]
            for s in slots:
                part = jnp.dot(X[w, s, at, rows], W[w, s, rows], preferred_element_type=jnp.float32)
                total = part if total is None else total + part
            A[w, at] = total

    def up_cast(j):
        up_load[j].wait()
        W[0, 0, chunk[j]] = U[chunk[j]].astype(jnp.bfloat16)

    x_local, x_send = [[], []], [[], []]

    def x_start():
        for w, src in enumerate((tok, cot)):
            for s in range(8):
                mine = pl.ds(pl.multiple_of(shard_at(s % 4, s // 4, c) * ROWS, ROWS), ROWS)
                its = pl.ds(pl.multiple_of(shard_at(s % 4, s // 4, 1 - c) * ROWS, ROWS), ROWS)
                copy = pltpu.make_async_copy(src.at[0, :, mine], X.at[w, s, pl.ds(0, TOK)], x_sem.at[w, s])
                copy.start()
                x_local[w].append(copy)
                x_send[w].append(
                    send(src.at[0, :, its], X.at[w, s, pl.ds(TOK, TOK)], xs_sem.at[w, s], xr_sem.at[w, s], partner)
                )
        dn_load.start()
        for copy in late:
            copy.start()

    def x_wait(w):
        for s in range(8):
            x_local[w][s].wait()
            x_send[w][s].wait_recv()
        if w == 1:
            dn_load.wait()

    near, far = (0, 1, 3, 4), (2, 5, 6, 7)
    partial, hidden = {}, {}

    def act():
        @pl.loop(0, 2)
        def _(t):
            at = pl.ds(pl.multiple_of(t * 128, 128), 128)
            v = (A[0, at] + R[0, at]) * D ** (-0.5)
            R[0, at] = v
            act = 0.5 * v * (1.0 + jnp.tanh(GELU_K * (v + GELU_C * (v * v * v))))
            G[1, 0, :, at] = act.T.astype(jnp.bfloat16)

    def grad():
        @pl.loop(0, 2)
        def _(t):
            at = pl.ds(pl.multiple_of(t * 128, 128), 128)
            upstream = (A[1, at] + R[1, at]) * FFW ** (-0.5)
            v = R[0, at]
            squared = v * v
            th = jnp.tanh(GELU_K * (v + GELU_C * (v * squared)))
            slope = 0.5 * (1.0 + th) + 0.5 * v * (1.0 - th * th) * (GELU_K * (1.0 + 3.0 * GELU_C * squared))
            G[0, 0, :, at] = (upstream * slope).T.astype(jnp.bfloat16)

    def swap_partial(w):
        partial[w] = send(A.at[w, pl.ds(TOK, TOK)], R.at[w], ps.at[w], pr.at[w], partner)

    def swap_hidden(w):
        hidden[w] = send(G.at[w, 0], G.at[w, 1], gs.at[w], gr.at[w], partner)

    def terms(w, j):
        rows = pl.ds(j * CH, CH)
        scale = D ** (-0.5) if w == 0 else FFW ** (-0.5)

        @pl.loop(0, 8)
        def _(s):
            part = jnp.dot(G[w, 0], X[w, s, pl.ds(0, TOK), rows], preferred_element_type=jnp.float32)
            part += jnp.dot(G[w, 1], X[w, s, pl.ds(TOK, TOK), rows], preferred_element_type=jnp.float32)
            T[w, j, s] = (part * scale).astype(jnp.bfloat16)

        if (w, j) == (1, LAST):
            E[3] = T[w, j, 0]

    rs = {}

    def rs_send(w, j, k, src, dst, to):
        rs[w, j, k] = send(src, dst, rss.at[w, j, k], rsr.at[w, j, k], to)

    low, high, full = pl.ds(0, HALF_F), pl.ds(HALF_F, HALF_F), pl.ds(0, FFW)

    def home(w, j, k):
        return E.at[k - 4] if (w, j) == (1, LAST) else B.at[w, j, k]

    def rs_one_z(w, j):
        rs_send(w, j, 0, T.at[w, j, 6], B.at[w, j, 0], zp)

    def rs_one_y(w, j):
        by_z = RS_Z.get((w, j), 0)
        to_yp, to_ym = pl.ds(0, FFW - by_z), pl.ds(by_z, FFW - by_z)
        rs_send(w, j, 1, T.at[w, j, 5, to_yp], B.at[w, j, 1, to_yp], yp)
        rs_send(w, j, 2, T.at[w, j, 7, to_ym], B.at[w, j, 2, to_ym], ym)
        if by_z:
            first, last = pl.ds(0, by_z), pl.ds(FFW - by_z, by_z)
            rs_send(w, j, 8, T.at[w, j, 5, last], B.at[w, j, 7, last], zp)
            rs_send(w, j, 9, T.at[w, j, 7, first], B.at[w, j, 7, first], zp)

    def add(w, j, slot, rows, *held):
        total = T[w, j, slot, rows].astype(jnp.float32)
        for k in held:
            total += B[w, j, k, rows].astype(jnp.float32)
        T[w, j, slot, rows] = total.astype(jnp.bfloat16)

    def rs_two_y(w, j):
        rs[w, j, 0].wait_recv()
        add(w, j, 2, full, 0)
        rs_send(w, j, 3, T.at[w, j, 2, low], B.at[w, j, 3, low], yp)
        rs_send(w, j, 4, T.at[w, j, 2, high], B.at[w, j, 3, high], ym)

    def rs_two_z(w, j):
        by_z = RS_Z.get((w, j), 0)
        rs[w, j, 1].wait_recv()
        rs[w, j, 2].wait_recv()
        if by_z:
            add(w, j, 4, pl.ds(0, by_z), 1)
            add(w, j, 4, pl.ds(FFW - by_z, by_z), 2)
        if by_z < HALF_F:
            add(w, j, 4, pl.ds(by_z, FFW - 2 * by_z), 1, 2)
        rs_send(w, j, 5, T.at[w, j, 4], home(w, j, 4), zp)

    def rs_three_a(w, j):
        by_z = RS_Z.get((w, j), 0)
        if by_z:
            rs[w, j, 8].wait_recv()
            add(w, j, 1, pl.ds(FFW - by_z, by_z), 7)
            rs[w, j, 9].wait_recv()
            add(w, j, 3, pl.ds(0, by_z), 7)
        rs_send(w, j, 10, T.at[w, j, 1, high], home(w, j, 5).at[high], yp)
        rs_send(w, j, 11, T.at[w, j, 3, low], home(w, j, 6).at[low], ym)

    def rs_three_b(w, j):
        rs[w, j, 3].wait_recv()
        add(w, j, 1, low, 3)
        rs_send(w, j, 6, T.at[w, j, 1, low], home(w, j, 5).at[low], yp)
        rs[w, j, 4].wait_recv()
        add(w, j, 3, high, 3)
        rs_send(w, j, 7, T.at[w, j, 3, high], home(w, j, 6).at[high], ym)

    def rs_four(w, j):
        for k in (5, 6, 7, 10, 11):
            rs[w, j, k].wait_recv()
        total = T[w, j, 0].astype(jnp.float32)
        for k in (4, 5, 6):
            total += B[w, j, k].astype(jnp.float32)
        return total.T

    ar = {}

    def adam(j):
        rows = pl.ds(j * CH, CH)
        grad = rs_four(0, j)
        first = beta_one * o_m1[rows] + (1.0 - beta_one) * grad
        o_m1[rows] = first
        second = beta_two * o_m2[rows] + (1.0 - beta_two) * grad * grad
        o_m2[rows] = second
        master = U[rows]
        stepped = master - inner_rate * (
            first / fix_one / (jnp.sqrt(second / fix_two) + adam_eps) + decay_rate * master
        )
        PS[j] = (o_anc[rows] - stepped).astype(jnp.bfloat16)
        for p in range(1, N_X):
            piece = pl.ds(pl.multiple_of(((x + p) % N_X) * PIECE, PIECE), PIECE)
            ar[j, p] = send(PS.at[j, piece], PR.at[j, N_X - p], ars.at[j, p], arr.at[j, N_X - p], beside[p])

    mean = {}

    def sum_x(j):
        for p in range(1, N_X):
            ar[j, p].wait_recv()
        total = PS[j, pl.ds(pl.multiple_of(x * PIECE, PIECE), PIECE)].astype(jnp.float32)
        for p in range(1, N_X):
            total += PR[j, p].astype(jnp.float32)
        PR[j, 0] = total.astype(jnp.bfloat16)
        ar[j, 0] = send(PR.at[j, 0], PR.at[j, N_X], ars.at[j, 0], arr.at[j, 0], above)

    def sum_z(j):
        ar[j, 0].wait_recv()
        mine = pl.ds(pl.multiple_of(x * PIECE, PIECE), PIECE)
        total = PR[j, 0].astype(jnp.float32) + PR[j, N_X].astype(jnp.float32)
        MN[j, mine] = (total / N_REP).astype(jnp.bfloat16)
        for p in range(1, N_X):
            mean[j, p] = send(MN.at[j, mine], MN.at[j, mine], mns.at[j, p], mnr.at[j, N_X - p], beside[p])

    def outer(j):
        rows = pl.ds(j * CH, CH)
        for p in range(1, N_X):
            mean[j, p].wait_recv()
        outer_mean = MN[j].astype(jnp.float32)
        new_momentum = outer_mu * o_mom[rows] + outer_mean
        o_mom[rows] = new_momentum
        o_anc[rows] = o_anc[rows] - outer_rate * (outer_mean + outer_mu * new_momentum)

    def tail(j):
        for k in (5, 6, 7, 10, 11):
            rs[1, j, k].wait_recv()

    def down(j):
        rows = pl.ds(j * CH, CH)
        o_acc[rows] = o_acc[rows] + rs_four(1, j)

    ag_own_y(1, 1)
    ag_own_z(1, 1)
    up_cast(1)
    ag_own_y(0, 1)
    up_cast(0)
    ag_own_z(0, 1)
    up_cast(2)
    x_start()
    ag_own_z(0, 2)
    ag_own_y(0, 0)
    ag_half(0, 1)
    ag_far(0, 1)
    ag_own_z(1, 0)
    ag_own_y(0, 2)
    ag_half(1, 1)
    ag_own_z(0, 0)
    ag_last(0, 1)
    ag_own_y(1, 0)
    ag_half(0, 0)
    ag_half(0, 2)
    ag_far(0, 0)
    ag_end(0, 1)
    x_wait(0)
    ag_half(1, 0)
    ag_own_y(1, 2)
    ag_last(0, 0)
    forward(0, 1, far)
    ag_far(0, 2)
    forward(0, 0, near)
    ag_far(1, 0)
    x_wait(1)
    forward(1, 0, near)
    forward(0, 1, near)
    ag_last(0, 2)
    ag_last(1, 0)
    ag_half(1, 2)
    ag_far(1, 1)
    forward(1, 1, near)
    ag_own_z(1, 2)
    forward(0, 2, near)
    ag_end(0, 0)
    ag_end(0, 2)
    ag_last(1, 1)
    forward(0, 2, far)
    forward(0, 0, far)
    swap_partial(0)
    partial[0].wait_recv()
    ag_end(1, 0)
    act()
    swap_hidden(1)
    ag_last(1, 2)
    forward(1, 0, far)
    hidden[1].wait_recv()
    ag_far(1, 2)
    forward(1, 2, near)
    terms(1, 0)
    terms(1, 1)
    rs_three_a(1, 1)
    rs_one_z(1, 0)
    ag_end(1, 1)
    forward(1, 1, far)
    rs_one_y(1, 1)
    rs_one_z(1, 1)
    rs_one_y(1, 0)
    ag_end(1, 2)
    forward(1, 2, far)
    swap_partial(1)
    partial[1].wait_recv()
    grad()
    swap_hidden(0)
    hidden[0].wait_recv()
    terms(0, 2)
    rs_one_z(0, 2)
    rs_one_y(0, 2)
    terms(0, 1)
    rs_one_y(0, 1)
    rs_one_z(0, 1)
    terms(0, 0)
    rs_three_a(0, 2)
    rs_one_z(0, 0)
    rs_two_z(0, 2)
    terms(1, 2)
    rs_two_y(0, 2)
    rs_one_y(0, 0)
    rs_two_y(0, 1)
    rs_three_b(0, 2)
    rs_two_y(0, 0)
    rs_three_b(0, 1)
    rs_two_z(0, 1)
    rs_two_z(0, 0)
    rs_three_a(0, 1)
    for copy in late:
        copy.wait()
    adam(2)
    rs_three_a(0, 0)
    rs_three_b(0, 0)
    rs_one_z(1, 2)
    rs_two_z(1, 0)
    rs_two_y(1, 0)
    rs_one_y(1, 2)
    adam(1)
    sum_x(2)
    adam(0)
    early = len(sends)
    rs_three_b(1, 0)
    rs_two_y(1, 1)
    sum_x(1)
    sum_z(2)
    rs_three_a(1, 0)
    rs_two_z(1, 1)
    rs_two_y(1, 2)
    sum_x(0)
    rs_three_a(1, 2)
    rs_two_z(1, 2)
    sum_z(1)
    rs_three_b(1, 1)
    sum_z(0)
    rs_three_b(1, 2)
    for copy in sends[:early]:
        copy.wait_send()
    outer(2)
    down(0)
    outer(1)
    down(1)
    outer(0)
    tail(2)
    for copy in sends[early:]:
        copy.wait_send()


def place(anc, mom, m1, m2, acc, E, o_anc, o_mom, o_m1, o_m2, o_acc, S, sem):
    pairs = ((m1, o_m1.at[0]), (m2, o_m2.at[0]), (acc, o_acc.at[0]), (anc, o_anc), (mom, o_mom))
    chunk = [pl.ds(j * CH, CH) for j in range(NCH)]
    copies = [
        pltpu.make_async_copy(src.at[chunk[j]], dst.at[chunk[j]], sem.at[i, j])
        for i, (src, dst) in enumerate(pairs)
        for j in range(NCH)
        if (i, j) != (2, LAST)
    ]
    for copy in copies:
        copy.start()
    total = E[3].astype(jnp.float32)
    for k in range(3):
        total += E[k].astype(jnp.float32)
    S[...] = acc[chunk[LAST]] + total.T
    copies.append(pltpu.make_async_copy(S, o_acc.at[0, chunk[LAST]], sem.at[2, LAST]))
    copies[-1].start()
    for copy in copies:
        copy.wait()


def on_device(tokens, cotangent, inner_up, adam_first, adam_second, inner_down, down_accum, anchor_up, outer_momentum):
    flat = jax.ShapeDtypeStruct((ROWS, FFW), jnp.float32)
    deep = jax.ShapeDtypeStruct((1, ROWS, FFW), jnp.float32)
    dma = pltpu.SemaphoreType.DMA
    bf16, f32 = jnp.bfloat16, jnp.float32
    held = pl.pallas_call(
        kernel,
        out_shape=(pltpu.VMEM((ROWS, FFW), f32),) * 5 + (pltpu.VMEM((4, FFW, CH), bf16),),
        in_specs=[pl.BlockSpec(memory_space=pl.ANY)] * 9,
        out_specs=[pl.BlockSpec(memory_space=pltpu.VMEM)] * 6,
        scratch_shapes=[
            pltpu.VMEM((2, 8, 2 * TOK, ROWS), bf16),
            pltpu.VMEM((2, 8, ROWS, FFW), bf16),
            pltpu.VMEM((2, 2 * TOK, FFW), f32),
            pltpu.VMEM((2, TOK, FFW), f32),
            pltpu.VMEM((2, 2, FFW, TOK), bf16),
            pltpu.VMEM((2, NCH, 8, FFW, CH), bf16),
            pltpu.VMEM((2, NCH, 8, FFW, CH), bf16),
            pltpu.VMEM((ROWS, FFW), f32),
            pltpu.VMEM((NCH, CH, FFW), bf16),
            pltpu.VMEM((NCH, N_X + 1, PIECE, FFW), bf16),
            pltpu.VMEM((NCH, CH, FFW), bf16),
            dma((9,)),
            dma((2, 8)),
            dma((2, 8)),
            dma((2, 8)),
            dma((2, NCH, 10)),
            dma((2, NCH, 10)),
            dma((2, NCH, 12)),
            dma((2, NCH, 12)),
            dma((2,)),
            dma((2,)),
            dma((2,)),
            dma((2,)),
            dma((NCH, N_X)),
            dma((NCH, N_X)),
            dma((NCH, N_X)),
            dma((NCH, N_X)),
        ],
        name="window",
        compiler_params=pltpu.CompilerParams(
            collective_id=0, has_side_effects=True, vmem_limit_bytes=50 * 2**20
        ),
        cost_estimate=pl.CostEstimate(flops=9_700_000_000, bytes_accessed=30_000_000, transcendentals=200_000),
    )(tokens, cotangent, inner_up, adam_first, adam_second, inner_down, down_accum, anchor_up, outer_momentum)
    return pl.pallas_call(
        place,
        out_shape=(flat, flat, deep, deep, deep),
        in_specs=[pl.BlockSpec(memory_space=pltpu.VMEM)] * 6,
        out_specs=[pl.BlockSpec(memory_space=pl.ANY)] * 5,
        scratch_shapes=[pltpu.VMEM((CH, FFW), f32), dma((5, NCH))],
        name="place",
        compiler_params=pltpu.CompilerParams(vmem_limit_bytes=4 * 2**20),
    )(*(pltpu.with_memory_space_constraint(value, pltpu.VMEM) for value in held))


def solution(mesh):
    return jax.shard_map(
        on_device,
        mesh=mesh,
        in_specs=(
            P("replica", "shard", None),
            P("replica", "shard", None),
            P("replica", "shard", None),
            P("replica", "shard", None),
            P("replica", "shard", None),
            P("replica", "shard", None),
            P("replica", "shard", None),
            P("shard", None),
            P("shard", None),
        ),
        out_specs=(
            P("shard", None),
            P("shard", None),
            P("replica", "shard", None),
            P("replica", "shard", None),
            P("replica", "shard", None),
        ),
        check_vma=False,
    )
```
